32 devices in a mesh: lon: 4 (over z), lat: 2 (over x), dp: 4 (over y, core).
Axes of the slice: x: 2, y: 2, z: 4, core: 2. Of those that a mesh axis runs over, the one named last changes fastest.
Arguments:
- fields: bfloat16 [4, 256, 16, 512], P('dp', None, 'lat', 'lon'), may hold values from -6 to 6
- weight_one: bfloat16 [9, 256, 256], replicated, may hold values from -0.125 to 0.125
- weight_two: bfloat16 [9, 256, 256], replicated, may hold values from -0.125 to 0.125
- edge_flips: int32 [1, 4], replicated, may hold values from 0 to 1, as said below
- cotangent: bfloat16 [4, 256, 16, 512], P('dp', None, 'lat', 'lon'), may hold values from -6 to 6
Outputs:
- output: bfloat16 [4, 256, 16, 512], P('dp', None, 'lat', 'lon')
- grad_fields: bfloat16 [4, 256, 16, 512], P('dp', None, 'lat', 'lon')
- grad_one: float32 [9, 256, 256], replicated
- grad_two: float32 [9, 256, 256], replicated
The draws below stay inside these ranges and needn't reach their ends.
Inputs may be any that keep to these rules, and one draw needn't show every extreme that they name: `edge_flips`: 0 on every edge inside a face; only row 2 // 2 - 1, the boundary between the band's two face rows, may hold 1, where the two faces meeting at that longitude tile store longitude in opposite orders.
All inputs are finite; a program needn't handle non-finite values.
Results may differ from the reference program's by a relative error of at most 0.0034.
Values may be sent and summed in bfloat16 or wider, within the bound.
A program may use at most 128 MiB of HBM per device.

```python
import jax
import jax.numpy as jnp

CH = 256
ROWS = 8
COLS = 128
BATCH = 4
LAT_CELLS = 16
LON_CELLS = 512
N_LON = 4
N_LAT = 2


def draw_edge_flips(key, part):
    first_key = jax.random.fold_in(key, 11)
    second_key = jax.random.fold_in(key, 12)
    random_bits = jax.random.randint(first_key, (N_LON,), 0, 2).astype(jnp.int32)
    chosen = jax.random.randint(second_key, (), 0, N_LON).astype(jnp.int32)
    columns = jnp.arange(N_LON, dtype=jnp.int32)
    line_flags = jnp.where(columns == chosen, 1, jnp.where(columns == (chosen + 1) % N_LON, 0, random_bits)).astype(jnp.int32)
    edge_rows = jnp.arange(N_LAT - 1, dtype=jnp.int32)[:, None]
    boundary = N_LAT // 2 - 1
    return jnp.where(edge_rows == boundary, line_flags[None, :], 0).astype(jnp.int32)


def shard_levels(own_key, shape, pieces, smallest, top_value):
    def one(position, blocks):
        steps = jax.random.uniform(jax.random.fold_in(jax.random.fold_in(own_key, 6), position), (blocks,), jnp.float32, smallest / len(pieces), top_value / len(pieces))
        return jnp.repeat(jnp.exp(steps), shape[position] // blocks).reshape((-1,) + (1,) * (len(shape) - position - 1))

    level = one(*pieces[0])
    for cut in pieces[1:]:
        level = level * one(*cut)
    return level


def centred(rng, shape, scale, reach, shards=(), kind=jnp.bfloat16):
    entries = jax.random.normal(rng, shape, jnp.float32) * scale
    if len(shards) > 0:
        entries = shard_levels(rng, shape, shards, -0.22, 0.18) * entries
    return jnp.clip(entries, min=-reach, max=reach).astype(kind)


def setup_inputs(seed: int = 0) -> dict:
    seeds = jax.random.split(jax.random.key(seed), 6)
    return {
        "fields": centred(seeds[0], (BATCH, CH, LAT_CELLS, LON_CELLS), 1.0, 6.0, ((0, 4), (2, 2), (3, 4))),
        "weight_one": centred(seeds[1], (9, CH, CH), (9 * CH) ** -0.5, 0.125),
        "weight_two": centred(seeds[2], (9, CH, CH), (9 * CH) ** -0.5, 0.125),
        "edge_flips": draw_edge_flips(jax.random.fold_in(seeds[5], 71), 0),
        "cotangent": centred(seeds[4], (BATCH, CH, LAT_CELLS, LON_CELLS), 1.0, 6.0, ((0, 4), (2, 2), (3, 4))),
    }


def tiles_of(source):
    batch, chans = (source.shape[0], source.shape[1])
    shaped = source.reshape(batch, chans, N_LAT, ROWS, N_LON, COLS)
    return jnp.transpose(shaped, (2, 4, 0, 1, 3, 5))

def field_of(tiles):
    batch, chans = (tiles.shape[2], tiles.shape[3])
    shaped = jnp.transpose(tiles, (2, 3, 0, 4, 1, 5))
    return shaped.reshape(batch, chans, N_LAT * ROWS, N_LON * COLS)

def pad_tiles(tiles, edge_flips):
    west = jnp.roll(tiles[..., -1:], 1, axis=1)
    east = jnp.roll(tiles[..., :1], -1, axis=1)
    extended = jnp.concatenate([west, tiles, east], -1)
    reverse = edge_flips[:, :, None, None, None]
    north_src = extended[:-1, :, :, :, -1, :]
    top_rim = jnp.where(reverse == 1, jnp.flip(north_src, -1), north_src)
    top_rim = jnp.concatenate([jnp.zeros_like(top_rim[:1]), top_rim], 0)
    south_src = extended[1:, :, :, :, 0, :]
    bottom = jnp.where(reverse == 1, jnp.flip(south_src, -1), south_src)
    bottom = jnp.concatenate([bottom, jnp.zeros_like(bottom[:1])], 0)
    return jnp.concatenate([top_rim[..., None, :], extended, bottom[..., None, :]], -2)

def convolve(padded_in, weight):
    total = None
    for tap_row in range(3):
        for tap_col in range(3):
            piece = padded_in[..., tap_row:tap_row + ROWS, tap_col:tap_col + COLS].astype(jnp.float32)
            term = jnp.einsum('oc,anbchw->anbohw', weight[3 * tap_row + tap_col].astype(jnp.float32), piece)
            total = term if total is None else total + term
    return total

def transposed(grad_tiles, weight):
    shape = grad_tiles.shape[:-2] + (ROWS + 2, COLS + 2)
    padded_grad = jnp.zeros(shape, jnp.float32)
    for tap_row in range(3):
        for tap_col in range(3):
            term = jnp.einsum('oc,anbohw->anbchw', weight[3 * tap_row + tap_col].astype(jnp.float32), grad_tiles.astype(jnp.float32))
            padded_grad = padded_grad.at[..., tap_row:tap_row + ROWS, tap_col:tap_col + COLS].add(term)
    return padded_grad

def kernel_grad(grad_tiles, padded_in):
    taps = []
    for tap_row in range(3):
        for tap_col in range(3):
            piece = padded_in[..., tap_row:tap_row + ROWS, tap_col:tap_col + COLS].astype(jnp.float32)
            taps.append(jnp.einsum('anbohw,anbchw->oc', grad_tiles.astype(jnp.float32), piece))
    return jnp.stack(taps, 0)

def reference(fields, weight_one, weight_two, edge_flips, cotangent):
    tile_view = tiles_of(fields)
    padded_in = pad_tiles(tile_view, edge_flips)
    hidden = convolve(padded_in, weight_one)
    activation = jax.nn.silu(hidden).astype(jnp.bfloat16)
    padded_act = pad_tiles(activation, edge_flips)
    output = (tile_view.astype(jnp.float32) + convolve(padded_act, weight_two)).astype(jnp.bfloat16)
    cot_tiles = tiles_of(cotangent)
    grad_two = kernel_grad(cot_tiles, padded_act)
    _, pullback = jax.vjp(lambda source: pad_tiles(source, edge_flips), jnp.zeros(tile_view.shape, jnp.float32))
    back_act = pullback(transposed(cot_tiles, weight_two))[0]
    sigmoid_h = jax.nn.sigmoid(hidden)
    back_hidden = (back_act * sigmoid_h * (1.0 + hidden * (1.0 - sigmoid_h))).astype(jnp.bfloat16)
    grad_one = kernel_grad(back_hidden, padded_in)
    grad_tiles = cot_tiles.astype(jnp.float32) + pullback(transposed(back_hidden, weight_one))[0]
    return (field_of(output), field_of(grad_tiles.astype(jnp.bfloat16)), grad_one, grad_two)
```

```python
import functools

import jax
import jax.numpy as jnp
from jax import lax
from jax.experimental import pallas as pl
from jax.experimental.pallas import tpu as pltpu
from jax.sharding import PartitionSpec as P

F32 = jnp.float32
BF16 = jnp.bfloat16
NN = (((1,), (0,)), ((), ()))
NT = (((1,), (1,)), ((), ()))
SIDES = ("W", "E", "U", "D", "UW", "UE", "DW", "DE")


def product(a, b, dims):
    return lax.dot_general(a, b, dims, preferred_element_type=F32)


def kernel(
    sizes,
    x_ref, g_ref, w1_ref, w2_ref, flip_ref,
    out_ref, gf_ref, o1_ref, o2_ref,
    x1, x2, gz, bz, gt, bt, q, hid, act,
    cell_out, cell_in, row_out, row_in,
    s0, a0, r0, s1, a1, r1, s2, a2, r2, near,
    halo_send, halo_recv, sum_send, sum_recv,
):
    n_lon, n_lat, n_dp, rows, cols, ch = sizes
    cells = rows * cols
    ny = n_dp // 2
    lon, lat, dp = lax.axis_index("lon"), lax.axis_index("lat"), lax.axis_index("dp")
    core, y = lax.rem(dp, 2), lax.div(dp, 2)
    west, east = lax.rem(lon + n_lon - 1, n_lon), lax.rem(lon + 1, n_lon)
    has_up, has_down = lat > 0, lat < n_lat - 1
    up, down = jnp.maximum(lat - 1, 0), jnp.minimum(lat + 1, n_lat - 1)

    cell_in[...] = jnp.zeros_like(cell_in)
    cell_out[...] = jnp.zeros_like(cell_out)
    row_in[...] = jnp.zeros_like(row_in)
    barrier = pltpu.get_barrier_semaphore()
    greeted = 0
    for i in range(n_lon):
        for j in range(n_lat):
            if i or j:
                pl.semaphore_signal(
                    barrier, inc=1,
                    device_id={"lon": lax.rem(lon + i, n_lon), "lat": lax.rem(lat + j, n_lat), "dp": dp},
                    device_id_type=pl.DeviceIdType.MESH,
                )
                greeted += 1
    for k in range(1, n_dp):
        pl.semaphore_signal(
            barrier, inc=1,
            device_id={"lon": lon, "lat": lat, "dp": lax.rem(dp + k, n_dp)},
            device_id_type=pl.DeviceIdType.MESH,
        )
        greeted += 1

    def remote(src, dst, send, recv, to_lon, to_lat, to_dp):
        return pltpu.make_async_remote_copy(
            src_ref=src, dst_ref=dst, send_sem=send, recv_sem=recv,
            device_id={"lon": to_lon, "lat": to_lat, "dp": to_dp},
            device_id_type=pl.DeviceIdType.MESH,
        )

    opposite = {"W": "E", "E": "W", "U": "D", "D": "U", "UW": "DE", "UE": "DW", "DW": "UE", "DE": "UW"}

    def halo_copy(e, side):
        to_lon = west if "W" in side else east if "E" in side else lon
        to_lat = up if "U" in side else down if "D" in side else lat
        slot, there = SIDES.index(side), SIDES.index(opposite[side])
        if side in ("U", "D"):
            src, dst = row_out.at[e, slot - 2], row_in.at[e, there - 2]
        else:
            src, dst = cell_out.at[e, slot], cell_in.at[e, there]
        return remote(src, dst, halo_send.at[e, slot], halo_recv.at[e, there], to_lon, to_lat, dp)

    def guarded(side, action):
        if "U" in side:
            pl.when(has_up)(action)
        elif "D" in side:
            pl.when(has_down)(action)
        else:
            action()

    def halo_start(e):
        for side in ("U", "D", "W", "E", "UW", "UE", "DW", "DE"):
            copy = halo_copy(e, side)
            guarded(side, copy.start)

    def halo_wait(e):
        for side in SIDES:
            copy = halo_copy(e, side)
            guarded(side, copy.wait_send)
            guarded(opposite[side], copy.wait_recv)

    line = lax.broadcasted_iota(jnp.int32, (cols, ch), 0)
    ja = lax.broadcasted_iota(jnp.int32, (cols, cols), 0)
    jb = lax.broadcasted_iota(jnp.int32, (cols, cols), 1)
    exchange = jnp.where(ja + jb == cols - 1, 1.0, 0.0).astype(BF16)
    flip_up, flip_down = flip_ref[0:1, :] > 0.5, flip_ref[8:9, :] > 0.5

    def turned(flag, west_cell, middle, east_cell):
        back = product(exchange, middle, NN)
        return (
            jnp.where(flag, east_cell, west_cell),
            jnp.where(flag, back, middle.astype(F32)),
            jnp.where(flag, west_cell, east_cell),
        )

    def send_field(e, ref):
        for h in range(rows):
            top = ref[h * cols : h * cols + 16, :].astype(F32)
            low = ref[(h + 1) * cols - 16 : (h + 1) * cols, :].astype(F32)
            cell_out[e, 0, h : h + 1, :] = top[0:1]
            cell_out[e, 1, h : h + 1, :] = low[15:16]
            if h == 0:
                cell_out[e, 4, 0:1, :] = top[0:1]
                cell_out[e, 5, 0:1, :] = low[15:16]
            if h == rows - 1:
                cell_out[e, 6, 0:1, :] = top[0:1]
                cell_out[e, 7, 0:1, :] = low[15:16]
        row_out[e, 0] = ref[0:cols, :]
        row_out[e, 1] = ref[cells - cols : cells, :]
        halo_start(e)

    def put_row(buf, i, west_cell, middle, east_cell):
        at = slice(i * cols, (i + 1) * cols)
        buf[at, 0:ch] = jnp.where(line == 0, west_cell, pltpu.roll(middle, 1, 0)).astype(BF16)
        buf[at, ch : 2 * ch] = middle.astype(BF16)
        buf[at, 2 * ch : 3 * ch] = jnp.where(
            line == cols - 1, east_cell, pltpu.roll(middle, cols - 1, 0)
        ).astype(BF16)

    def pad_field(e, ref, buf):
        halo_wait(e)
        for h in range(rows):
            put_row(
                buf, h + 1, cell_in[e, 0, h : h + 1, :],
                ref[h * cols : (h + 1) * cols, :].astype(F32), cell_in[e, 1, h : h + 1, :],
            )
        put_row(buf, 0, *turned(flip_up, cell_in[e, 4, 0:1, :], row_in[e, 0], cell_in[e, 5, 0:1, :]))
        put_row(buf, rows + 1, *turned(flip_down, cell_in[e, 6, 0:1, :], row_in[e, 1], cell_in[e, 7, 0:1, :]))

    block = cells // 2

    def conv(buf, w_ref, i):
        left = jnp.concatenate(
            [buf[i * block + r * cols : i * block + r * cols + block, :] for r in range(3)], 1
        )
        right = jnp.concatenate([w_ref[t] for t in range(9)], 1)
        return product(left, right, NT)

    def back_conv(e, z, w_ref):
        step = (rows + 2) // 2
        size = step * cols
        for i in range(2):
            left = jnp.concatenate(
                [z[i * size + (2 - r) * cols : i * size + (2 - r) * cols + size, :] for r in range(3)], 1
            )
            ys = [
                product(left, jnp.concatenate([w_ref[3 * r + s] for r in range(3)], 0), NN)
                for s in range(3)
            ]
            for k in range(step):
                n = i * step + k
                at = slice(k * cols, (k + 1) * cols)
                y0, y1, y2 = ys[0][at], ys[1][at], ys[2][at]
                total = (
                    y1
                    + jnp.where(line == cols - 1, 0.0, pltpu.roll(y0, cols - 1, 0))
                    + jnp.where(line == 0, 0.0, pltpu.roll(y2, 1, 0))
                )
                if 0 < n < rows + 1:
                    q[(n - 1) * cols : n * cols, :] = total
                    cell_out[e, 0, n - 1 : n, :] = y0[0:1]
                    cell_out[e, 1, n - 1 : n, :] = y2[cols - 1 : cols]
                else:
                    flag, slot = (flip_up, 0) if n == 0 else (flip_down, 1)
                    first, middle, last = turned(
                        flag, y0[0:1], total.astype(BF16), y2[cols - 1 : cols]
                    )
                    row_out[e, slot] = middle.astype(BF16)
                    cell_out[e, 4 + 2 * slot, 0:1, :] = first
                    cell_out[e, 5 + 2 * slot, 0:1, :] = last
        halo_start(e)

    def returned_row(e, h):
        value = q[h * cols : (h + 1) * cols, :]
        west_cell, east_cell = cell_in[e, 0, h : h + 1, :], cell_in[e, 1, h : h + 1, :]
        if h == 0:
            value = value + row_in[e, 0].astype(F32)
            west_cell = west_cell + cell_in[e, 4, 0:1, :]
            east_cell = east_cell + cell_in[e, 5, 0:1, :]
        if h == rows - 1:
            value = value + row_in[e, 1].astype(F32)
            west_cell = west_cell + cell_in[e, 6, 0:1, :]
            east_cell = east_cell + cell_in[e, 7, 0:1, :]
        return value + jnp.where(line == 0, west_cell, 0.0) + jnp.where(line == cols - 1, east_cell, 0.0)

    part_rows = 3 * ch
    half, quarter = part_rows // 2, part_rows // (2 * ny)
    piece = quarter // n_lat

    def start_all(copies):
        for copy in copies:
            copy.start()

    def finish(copies):
        for copy in copies:
            copy.wait()

    def gathered(p):
        ref = o1_ref if p < 3 else o2_ref
        return lambda start, size: ref.at[pl.ds(pl.multiple_of((p % 3) * part_rows + start, 16), size), :]

    core_at, y_at, lat_at = core * half, core * half + y * quarter, core * half + y * quarter + lat * piece
    slots = iter(range(1000))
    sem_core, sem_y, sem_lat, sem_lon, sem_lat2, sem_y2, sem_core2 = (
        [next(slots) for _ in range(n)] for n in (1, ny - 1, n_lat - 1, n_lon - 1, n_lat - 1, ny - 1, 1)
    )

    def to_core(p, src, dst, sem):
        return remote(src, dst, sum_send.at[p, sem], sum_recv.at[p, sem], lon, lat, y * 2 + 1 - core)

    def to_y(p, src, dst, sem, k):
        return remote(src, dst, sum_send.at[p, sem], sum_recv.at[p, sem], lon, lat, lax.rem(y + k, ny) * 2 + core)

    def to_lat(p, src, dst, sem, k):
        return remote(src, dst, sum_send.at[p, sem], sum_recv.at[p, sem], lon, lax.rem(lat + k, n_lat), dp)

    def to_lon(p, src, dst, sem, k):
        return remote(src, dst, sum_send.at[p, sem], sum_recv.at[p, sem], lax.rem(lon + k, n_lon), lat, dp)

    def rows_of(start, size):
        return pl.ds(pl.multiple_of(start, 16), size)

    def reduce_steps(p, grad):
        for s in range(3):
            a0[p, s * ch : (s + 1) * ch, :] = grad[:, s * ch : (s + 1) * ch]
            s0[p, s * ch : (s + 1) * ch, :] = grad[:, s * ch : (s + 1) * ch].astype(BF16)
        copies = [to_core(p, s0.at[p, rows_of((1 - core) * half, half), :], r0.at[p], sem_core[0])]
        start_all(copies)
        yield
        finish(copies)
        total = a0[p, rows_of(core_at, half), :] + r0[p].astype(F32)
        a1[p] = total
        s1[p] = total.astype(BF16)
        copies = [
            to_y(p, s1.at[p, rows_of(lax.rem(y + k, ny) * quarter, quarter), :], r1.at[p, k - 1], sem_y[k - 1], k)
            for k in range(1, ny)
        ]
        start_all(copies)
        yield
        finish(copies)
        total = a1[p, rows_of(y * quarter, quarter), :]
        for k in range(1, ny):
            total = total + r1[p, k - 1].astype(F32)
        a2[p] = total
        s2[p] = total.astype(BF16)
        copies = [
            to_lat(p, s2.at[p, rows_of(lax.rem(lat + k, n_lat) * piece, piece), :], r2.at[p, k - 1], sem_lat[k - 1], k)
            for k in range(1, n_lat)
        ]
        start_all(copies)
        yield
        finish(copies)
        total = a2[p, rows_of(lat * piece, piece), :]
        for k in range(1, n_lat):
            total = total + r2[p, k - 1].astype(F32)
        near[p, lon] = total.astype(BF16)
        copies = [to_lon(p, near.at[p, lon], near.at[p, lon], sem_lon[k - 1], k) for k in range(1, n_lon)]
        start_all(copies)
        yield
        finish(copies)
        total = near[p, 0].astype(F32)
        for k in range(1, n_lon):
            total = total + near[p, k].astype(F32)
        place = gathered(p)
        mine = place(lat_at, piece)
        mine[...] = total.astype(BF16)
        copies = [to_lat(p, mine, mine, sem_lat2[k - 1], k) for k in range(1, n_lat)]
        start_all(copies)
        yield
        finish(copies)
        mine = place(y_at, quarter)
        copies = [to_y(p, mine, mine, sem_y2[k - 1], k) for k in range(1, ny)]
        start_all(copies)
        yield
        finish(copies)
        mine = place(core_at, half)
        copies = [to_core(p, mine, mine, sem_core2[0])]
        start_all(copies)
        yield
        finish(copies)

    running = []

    def tick():
        for steps in list(running):
            if next(steps, "end") == "end":
                running.remove(steps)

    def begin(p, grad):
        tick()
        steps = reduce_steps(p, grad)
        next(steps)
        running.append(steps)

    pl.semaphore_wait(barrier, greeted)
    send_field(0, x_ref)

    edge = jnp.zeros((2 * cols, ch), BF16)
    for z in (gz, bz):
        z[0 : 2 * cols, :] = edge
        z[2 * cols + cells : 4 * cols + cells, :] = edge
    for h in range(rows):
        value = g_ref[h * cols : (h + 1) * cols, :]
        gz[(h + 2) * cols : (h + 3) * cols, :] = value
        gt[:, h * cols : (h + 1) * cols] = value.astype(F32).T.astype(BF16)
    back_conv(2, gz, w2_ref)

    pad_field(0, x_ref, x1)
    for i in range(2):
        value = conv(x1, w1_ref, i)
        hid[i * block : (i + 1) * block, :] = value
        act[i * block : (i + 1) * block, :] = (value / (1.0 + jnp.exp(-value))).astype(BF16)
    send_field(1, act)

    halo_wait(2)
    for h in range(rows):
        back = returned_row(2, h)
        value = hid[h * cols : (h + 1) * cols, :]
        sigma = 1.0 / (1.0 + jnp.exp(-value))
        back = back * sigma * (1.0 + value * (1.0 - sigma))
        bz[(h + 2) * cols : (h + 3) * cols, :] = back.astype(BF16)
        bt[:, h * cols : (h + 1) * cols] = back.T.astype(BF16)

    for r in range(3):
        begin(r, product(bt[...], x1[r * cols : r * cols + cells, :], NN))
    pad_field(1, act, x2)
    for r in range(3):
        begin(3 + r, product(gt[...], x2[r * cols : r * cols + cells, :], NN))
    back_conv(3, bz, w1_ref)
    tick()
    for i in range(2):
        at = slice(i * block, (i + 1) * block)
        out_ref[at, :] = (x_ref[at, :].astype(F32) + conv(x2, w2_ref, i)).astype(BF16)
        tick()
    halo_wait(3)
    for h in range(rows):
        at = slice(h * cols, (h + 1) * cols)
        gf_ref[at, :] = (g_ref[at, :].astype(F32) + returned_row(3, h)).astype(BF16)
    while running:
        tick()


def per_device(sizes, fields, weight_one, weight_two, edge_flips, cotangent):
    n_lon, n_lat, n_dp = sizes
    _, ch, rows, cols = fields.shape
    cells = rows * cols
    ny = n_dp // 2
    lat, lon = lax.axis_index("lat"), lax.axis_index("lon")
    upper = lax.dynamic_slice(edge_flips, (jnp.maximum(lat - 1, 0), lon), (1, 1))
    lower = lax.dynamic_slice(edge_flips, (jnp.minimum(lat, n_lat - 2), lon), (1, 1))
    flips = jnp.concatenate(
        [jnp.broadcast_to(upper, (8, ch)), jnp.broadcast_to(lower, (8, ch))], 0
    ).astype(F32)

    def by_cells(array):
        return jnp.transpose(array[0], (1, 2, 0)).reshape(cells, ch)

    part, half = 3 * ch, 3 * ch // 2
    quarter = part // (2 * ny)
    piece = quarter // n_lat
    copies = 2 * ny + 2 * n_lat + n_lon
    vmem = pl.BlockSpec(memory_space=pltpu.VMEM)
    padded = ((rows + 2) * cols, part)
    zeroed = ((rows + 4) * cols, ch)
    out, grad_fields, grad_one, grad_two = pl.pallas_call(
        functools.partial(kernel, (n_lon, n_lat, n_dp, rows, cols, ch)),
        out_shape=[jax.ShapeDtypeStruct((cells, ch), BF16)] * 2
        + [jax.ShapeDtypeStruct((9 * ch, ch), BF16)] * 2,
        in_specs=[vmem] * 5,
        out_specs=[vmem] * 4,
        scratch_shapes=[
            pltpu.VMEM(padded, BF16), pltpu.VMEM(padded, BF16),
            pltpu.VMEM(zeroed, BF16), pltpu.VMEM(zeroed, BF16),
            pltpu.VMEM((ch, cells), BF16), pltpu.VMEM((ch, cells), BF16),
            pltpu.VMEM((cells, ch), F32), pltpu.VMEM((cells, ch), F32), pltpu.VMEM((cells, ch), BF16),
            pltpu.VMEM((4, 8, rows, ch), F32), pltpu.VMEM((4, 8, rows, ch), F32),
            pltpu.VMEM((4, 2, cols, ch), BF16), pltpu.VMEM((4, 2, cols, ch), BF16),
            pltpu.VMEM((6, part, ch), BF16), pltpu.VMEM((6, part, ch), F32), pltpu.VMEM((6, half, ch), BF16),
            pltpu.VMEM((6, half, ch), BF16), pltpu.VMEM((6, half, ch), F32), pltpu.VMEM((6, ny - 1, quarter, ch), BF16),
            pltpu.VMEM((6, quarter, ch), BF16), pltpu.VMEM((6, quarter, ch), F32), pltpu.VMEM((6, n_lat - 1, piece, ch), BF16),
            pltpu.VMEM((6, n_lon, piece, ch), BF16),
            pltpu.SemaphoreType.DMA((4, 8)), pltpu.SemaphoreType.DMA((4, 8)),
            pltpu.SemaphoreType.DMA((6, copies)), pltpu.SemaphoreType.DMA((6, copies)),
        ],
        compiler_params=pltpu.CompilerParams(
            collective_id=0, has_side_effects=True, vmem_limit_bytes=52 * 1024 * 1024
        ),
        cost_estimate=pl.CostEstimate(
            flops=12 * 9 * ch * ch * cells, bytes_accessed=8 * 9 * ch * ch, transcendentals=2 * cells * ch
        ),
    )(by_cells(fields), by_cells(cotangent), weight_one, weight_two, flips)

    def by_channels(array):
        return jnp.transpose(array.reshape(rows, cols, ch), (2, 0, 1))[None]

    return (
        by_channels(out),
        by_channels(grad_fields),
        grad_one.reshape(9, ch, ch).astype(F32),
        grad_two.reshape(9, ch, ch).astype(F32),
    )


def solution(mesh):
    tile = P("dp", None, "lat", "lon")
    sizes = tuple(mesh.shape[axis] for axis in ("lon", "lat", "dp"))
    return jax.shard_map(
        functools.partial(per_device, sizes), mesh=mesh,
        in_specs=(tile, P(), P(), P(), tile), out_specs=(tile, tile, P(), P()), check_vma=False,
    )
```

```python
import functools

import jax
import jax.numpy as jnp
from jax import lax
from jax.experimental import pallas as pl
from jax.experimental.pallas import tpu as pltpu
from jax.sharding import PartitionSpec as P

F32 = jnp.float32
BF16 = jnp.bfloat16
NN = (((1,), (0,)), ((), ()))
NT = (((1,), (1,)), ((), ()))
SIDES = ("W", "E", "U", "D", "UW", "UE", "DW", "DE")


def product(a, b, dims):
    return lax.dot_general(a, b, dims, preferred_element_type=F32)


def kernel(
    sizes,
    x_ref, g_ref, w1_ref, w2_ref, flip_ref,
    out_ref, gf_ref, o1_ref, o2_ref,
    x1, x2, gz, bz, gt, bt, q, hid, act,
    cell_out, cell_in, row_out, row_in,
    a0, r0, s1, a1, r1, s2, a2, r2, a3, r3, near, full,
    halo_send, halo_recv, sum_send, sum_recv,
):
    n_lon, n_lat, n_dp, rows, cols, ch = sizes
    cells = rows * cols
    ny = n_dp // 2
    lon, lat, dp = lax.axis_index("lon"), lax.axis_index("lat"), lax.axis_index("dp")
    core, y = lax.rem(dp, 2), lax.div(dp, 2)
    west, east = lax.rem(lon + n_lon - 1, n_lon), lax.rem(lon + 1, n_lon)
    has_up, has_down = lat > 0, lat < n_lat - 1
    up, down = jnp.maximum(lat - 1, 0), jnp.minimum(lat + 1, n_lat - 1)

    cell_in[...] = jnp.zeros_like(cell_in)
    cell_out[...] = jnp.zeros_like(cell_out)
    row_in[...] = jnp.zeros_like(row_in)
    barrier = pltpu.get_barrier_semaphore()
    greeted = 0
    for i in range(n_lon):
        for j in range(n_lat):
            if i or j:
                pl.semaphore_signal(
                    barrier, inc=1,
                    device_id={"lon": lax.rem(lon + i, n_lon), "lat": lax.rem(lat + j, n_lat), "dp": dp},
                    device_id_type=pl.DeviceIdType.MESH,
                )
                greeted += 1
    for k in range(1, n_dp):
        pl.semaphore_signal(
            barrier, inc=1,
            device_id={"lon": lon, "lat": lat, "dp": lax.rem(dp + k, n_dp)},
            device_id_type=pl.DeviceIdType.MESH,
        )
        greeted += 1

    def remote(src, dst, send, recv, to_lon, to_lat, to_dp):
        return pltpu.make_async_remote_copy(
            src_ref=src, dst_ref=dst, send_sem=send, recv_sem=recv,
            device_id={"lon": to_lon, "lat": to_lat, "dp": to_dp},
            device_id_type=pl.DeviceIdType.MESH,
        )

    opposite = {"W": "E", "E": "W", "U": "D", "D": "U", "UW": "DE", "UE": "DW", "DW": "UE", "DE": "UW"}

    def halo_copy(e, side):
        to_lon = west if "W" in side else east if "E" in side else lon
        to_lat = up if "U" in side else down if "D" in side else lat
        slot, there = SIDES.index(side), SIDES.index(opposite[side])
        if side in ("U", "D"):
            src, dst = row_out.at[e, slot - 2], row_in.at[e, there - 2]
        else:
            src, dst = cell_out.at[e, slot], cell_in.at[e, there]
        return remote(src, dst, halo_send.at[e, slot], halo_recv.at[e, there], to_lon, to_lat, dp)

    def guarded(side, action):
        if "U" in side:
            pl.when(has_up)(action)
        elif "D" in side:
            pl.when(has_down)(action)
        else:
            action()

    def halo_start(e):
        for side in ("U", "D", "W", "E", "UW", "UE", "DW", "DE"):
            copy = halo_copy(e, side)
            guarded(side, copy.start)

    def halo_wait(e):
        for side in SIDES:
            copy = halo_copy(e, side)
            guarded(side, copy.wait_send)
            guarded(opposite[side], copy.wait_recv)

    line = lax.broadcasted_iota(jnp.int32, (cols, ch), 0)
    ja = lax.broadcasted_iota(jnp.int32, (cols, cols), 0)
    jb = lax.broadcasted_iota(jnp.int32, (cols, cols), 1)
    exchange = jnp.where(ja + jb == cols - 1, 1.0, 0.0).astype(BF16)
    zero = jnp.zeros((1, ch), jnp.int32)
    flip_up = zero + flip_ref[jnp.maximum(lat - 1, 0), lon] == 1
    flip_down = zero + flip_ref[jnp.minimum(lat, n_lat - 2), lon] == 1

    def turned(flag, west_cell, middle, east_cell):
        back = product(exchange, middle, NN)
        return (
            jnp.where(flag, east_cell, west_cell),
            jnp.where(flag, back, middle.astype(F32)),
            jnp.where(flag, west_cell, east_cell),
        )

    def send_field(e, ref):
        for h in range(rows):
            top = ref[h * cols : h * cols + 16, :].astype(F32)
            low = ref[(h + 1) * cols - 16 : (h + 1) * cols, :].astype(F32)
            cell_out[e, 0, h : h + 1, :] = top[0:1]
            cell_out[e, 1, h : h + 1, :] = low[15:16]
            if h == 0:
                cell_out[e, 4, 0:1, :] = top[0:1]
                cell_out[e, 5, 0:1, :] = low[15:16]
            if h == rows - 1:
                cell_out[e, 6, 0:1, :] = top[0:1]
                cell_out[e, 7, 0:1, :] = low[15:16]
        row_out[e, 0] = ref[0:cols, :]
        row_out[e, 1] = ref[cells - cols : cells, :]
        halo_start(e)

    def put_row(buf, i, west_cell, middle, east_cell):
        at = slice(i * cols, (i + 1) * cols)
        buf[at, 0:ch] = jnp.where(line == 0, west_cell, pltpu.roll(middle, 1, 0)).astype(BF16)
        buf[at, ch : 2 * ch] = middle.astype(BF16)
        buf[at, 2 * ch : 3 * ch] = jnp.where(
            line == cols - 1, east_cell, pltpu.roll(middle, cols - 1, 0)
        ).astype(BF16)

    def pad_field(e, ref, buf):
        halo_wait(e)
        for h in range(rows):
            put_row(
                buf, h + 1, cell_in[e, 0, h : h + 1, :],
                ref[h * cols : (h + 1) * cols, :].astype(F32), cell_in[e, 1, h : h + 1, :],
            )
        put_row(buf, 0, *turned(flip_up, cell_in[e, 4, 0:1, :], row_in[e, 0], cell_in[e, 5, 0:1, :]))
        put_row(buf, rows + 1, *turned(flip_down, cell_in[e, 6, 0:1, :], row_in[e, 1], cell_in[e, 7, 0:1, :]))

    block = cells // 2

    def conv(buf, w_ref, i):
        left = jnp.concatenate(
            [buf[i * block + r * cols : i * block + r * cols + block, :] for r in range(3)], 1
        )
        right = jnp.concatenate([w_ref[t] for t in range(9)], 1)
        return product(left, right, NT)

    def back_conv(e, z, w_ref):
        step = (rows + 2) // 2
        size = step * cols
        for i in range(2):
            left = jnp.concatenate(
                [z[i * size + (2 - r) * cols : i * size + (2 - r) * cols + size, :] for r in range(3)], 1
            )
            ys = [
                product(left, jnp.concatenate([w_ref[3 * r + s] for r in range(3)], 0), NN)
                for s in range(3)
            ]
            for k in range(step):
                n = i * step + k
                at = slice(k * cols, (k + 1) * cols)
                y0, y1, y2 = ys[0][at], ys[1][at], ys[2][at]
                total = (
                    y1
                    + jnp.where(line == cols - 1, 0.0, pltpu.roll(y0, cols - 1, 0))
                    + jnp.where(line == 0, 0.0, pltpu.roll(y2, 1, 0))
                )
                if 0 < n < rows + 1:
                    q[(n - 1) * cols : n * cols, :] = total
                    cell_out[e, 0, n - 1 : n, :] = y0[0:1]
                    cell_out[e, 1, n - 1 : n, :] = y2[cols - 1 : cols]
                else:
                    flag, slot = (flip_up, 0) if n == 0 else (flip_down, 1)
                    first, middle, last = turned(
                        flag, y0[0:1], total.astype(BF16), y2[cols - 1 : cols]
                    )
                    row_out[e, slot] = middle.astype(BF16)
                    cell_out[e, 4 + 2 * slot, 0:1, :] = first
                    cell_out[e, 5 + 2 * slot, 0:1, :] = last
            tick()
        halo_start(e)

    def returned_row(e, h):
        value = q[h * cols : (h + 1) * cols, :]
        west_cell, east_cell = cell_in[e, 0, h : h + 1, :], cell_in[e, 1, h : h + 1, :]
        if h == 0:
            value = value + row_in[e, 0].astype(F32)
            west_cell = west_cell + cell_in[e, 4, 0:1, :]
            east_cell = east_cell + cell_in[e, 5, 0:1, :]
        if h == rows - 1:
            value = value + row_in[e, 1].astype(F32)
            west_cell = west_cell + cell_in[e, 6, 0:1, :]
            east_cell = east_cell + cell_in[e, 7, 0:1, :]
        return value + jnp.where(line == 0, west_cell, 0.0) + jnp.where(line == cols - 1, east_cell, 0.0)

    lanes = ch // 2
    part_rows = 6 * ch
    half = part_rows // 2
    piece = half // (ny * n_lat)
    strip = piece // n_lon
    scattered = strip % 16 == 0

    def rows_of(start, size):
        return pl.ds(pl.multiple_of(start, 16), size)

    def reduce_steps(p, grad):
        target = full.at[p]
        sem = iter(range(1000))

        def send(src, dst, axis, k=1):
            slot = next(sem)
            to = {"lon": lon, "lat": lat, "dp": dp}
            if axis == "core":
                to["dp"] = y * 2 + 1 - core
            elif axis == "y":
                to["dp"] = lax.rem(y + k, ny) * 2 + core
            elif axis == "lat":
                to["lat"] = lax.rem(lat + k, n_lat)
            else:
                to["lon"] = lax.rem(lon + k, n_lon)
            copy = remote(
                src, dst, sum_send.at[p, slot], sum_recv.at[p, slot], to["lon"], to["lat"], to["dp"]
            )
            copy.start()
            return copy

        def finish(copies):
            for copy in copies:
                copy.wait()

        first, second = (("y", ny, y), ("lat", n_lat, lat))[:: 1 if p % 2 == 0 else -1]
        size1 = half // first[1]

        for n in range(6):
            a0[p, n * ch : (n + 1) * ch, :] = grad[:, n * lanes : (n + 1) * lanes]
        copies = [send(a0.at[p, rows_of((1 - core) * half, half), :], r0.at[p], "core")]
        yield
        finish(copies)
        total = a0[p, rows_of(core * half, half), :] + r0[p]
        a1[p] = total
        s1[p] = total.astype(BF16)
        axis, count, mine = first
        copies = [
            send(
                s1.at[p, rows_of(lax.rem(mine + k, count) * size1, size1), :],
                r1.at[p, (k - 1) * size1 : k * size1, :], axis, k,
            )
            for k in range(1, count)
        ]
        yield
        finish(copies)
        total = a1[p, rows_of(mine * size1, size1), :]
        for k in range(1, count):
            total = total + r1[p, (k - 1) * size1 : k * size1, :].astype(F32)
        a2[p, 0:size1, :] = total
        s2[p, 0:size1, :] = total.astype(BF16)
        axis, count, mine = second
        copies = [
            send(
                s2.at[p, rows_of(lax.rem(mine + k, count) * piece, piece), :],
                r2.at[p, (k - 1) * piece : k * piece, :], axis, k,
            )
            for k in range(1, count)
        ]
        yield
        finish(copies)
        total = a2[p, rows_of(mine * piece, piece), :]
        for k in range(1, count):
            total = total + r2[p, (k - 1) * piece : k * piece, :].astype(F32)
        at1 = core * half + first[2] * size1
        at2 = at1 + second[2] * piece
        if scattered:
            a3[p] = total
            copies = []
            for k in range(1, n_lon):
                there = rows_of(lax.rem(lon + k, n_lon) * strip, strip)
                copies.append(send(a3.at[p, there, :], r3.at[p, k - 1], "lon", k))
            yield
            finish(copies)
            total = a3[p, rows_of(lon * strip, strip), :]
            for k in range(1, n_lon):
                total = total + r3[p, k - 1]
            own = target.at[rows_of(at2 + lon * strip, strip), :]
            own[...] = total.astype(BF16)
            copies = [send(own, own, "lon", k) for k in range(1, n_lon)]
            yield
            finish(copies)
        else:
            near[p, lon] = total.astype(BF16)
            copies = [send(near.at[p, lon], near.at[p, lon], "lon", k) for k in range(1, n_lon)]
            yield
            finish(copies)
            total = near[p, 0].astype(F32)
            for k in range(1, n_lon):
                total = total + near[p, k].astype(F32)
            target[rows_of(at2, piece), :] = total.astype(BF16)
        own = target.at[rows_of(at2, piece), :]
        copies = [send(own, own, second[0], k) for k in range(1, second[1])]
        yield
        finish(copies)
        own = target.at[rows_of(at1, size1), :]
        copies = [send(own, own, first[0], k) for k in range(1, first[1])]
        yield
        finish(copies)
        own = target.at[rows_of(core * half, half), :]
        copies = [send(own, own, "core")]
        yield
        finish(copies)
        result = o1_ref if p < 3 else o2_ref
        for n in range(6):
            result[3 * (p % 3) + n // 2, :, (n % 2) * lanes : (n % 2 + 1) * lanes] = full[
                p, n * ch : (n + 1) * ch, :
            ]

    patience = (1, 3, 2, 2, 1, 1, 2, 1)
    running = []

    def tick():
        for state in list(running):
            state["age"] += 1
            if state["age"] >= patience[state["step"]]:
                state["age"], state["step"] = 0, state["step"] + 1
                if next(state["steps"], "end") == "end":
                    running.remove(state)

    def begin(p, grad):
        steps = reduce_steps(p, grad)
        next(steps)
        tick()
        running.append({"steps": steps, "age": 0, "step": 0})

    pl.semaphore_wait(barrier, greeted)
    send_field(0, x_ref)

    edge = jnp.zeros((2 * cols, ch), BF16)
    for z in (gz, bz):
        z[0 : 2 * cols, :] = edge
        z[2 * cols + cells : 4 * cols + cells, :] = edge
    for h in range(rows):
        value = g_ref[h * cols : (h + 1) * cols, :]
        gz[(h + 2) * cols : (h + 3) * cols, :] = value
        gt[:, h * cols : (h + 1) * cols] = value.astype(F32).T.astype(BF16)
    back_conv(2, gz, w2_ref)

    pad_field(0, x_ref, x1)
    for i in range(2):
        value = conv(x1, w1_ref, i)
        hid[i * block : (i + 1) * block, :] = value
        act[i * block : (i + 1) * block, :] = (value / (1.0 + jnp.exp(-value))).astype(BF16)
    send_field(1, act)

    halo_wait(2)
    for h in range(rows):
        back = returned_row(2, h)
        value = hid[h * cols : (h + 1) * cols, :]
        sigma = 1.0 / (1.0 + jnp.exp(-value))
        back = back * sigma * (1.0 + value * (1.0 - sigma))
        bz[(h + 2) * cols : (h + 3) * cols, :] = back.astype(BF16)
        bt[:, h * cols : (h + 1) * cols] = back.T.astype(BF16)

    for r in range(3):
        begin(r, product(bt[...], x1[r * cols : r * cols + cells, :], NN))
    pad_field(1, act, x2)
    tick()
    for r in range(3):
        begin(3 + r, product(gt[...], x2[r * cols : r * cols + cells, :], NN))
    back_conv(3, bz, w1_ref)
    for i in range(2):
        at = slice(i * block, (i + 1) * block)
        out_ref[at, :] = (x_ref[at, :].astype(F32) + conv(x2, w2_ref, i)).astype(BF16)
        tick()
    halo_wait(3)
    for h in range(rows):
        at = slice(h * cols, (h + 1) * cols)
        gf_ref[at, :] = (g_ref[at, :].astype(F32) + returned_row(3, h)).astype(BF16)
    patience = (1,) * 8
    while running:
        tick()


def per_device(sizes, fields, weight_one, weight_two, edge_flips, cotangent):
    n_lon, n_lat, n_dp = sizes
    _, ch, rows, cols = fields.shape
    cells = rows * cols
    ny = n_dp // 2
    def by_cells(array):
        return jnp.transpose(array[0], (1, 2, 0)).reshape(cells, ch)

    part, half, lanes = 3 * ch, 3 * ch, ch // 2
    piece = half // (ny * n_lat)
    strip = max(8, piece // n_lon)
    copies = 2 * (ny + n_lat + n_lon)
    vmem = pl.BlockSpec(memory_space=pltpu.VMEM)
    padded = ((rows + 2) * cols, part)
    zeroed = ((rows + 4) * cols, ch)
    out, grad_fields, grad_one, grad_two = pl.pallas_call(
        functools.partial(kernel, (n_lon, n_lat, n_dp, rows, cols, ch)),
        out_shape=[jax.ShapeDtypeStruct((cells, ch), BF16)] * 2
        + [jax.ShapeDtypeStruct((9, ch, ch), BF16)] * 2,
        in_specs=[vmem] * 4 + [pl.BlockSpec(memory_space=pltpu.SMEM)],
        out_specs=[vmem] * 4,
        scratch_shapes=[
            pltpu.VMEM(padded, BF16), pltpu.VMEM(padded, BF16),
            pltpu.VMEM(zeroed, BF16), pltpu.VMEM(zeroed, BF16),
            pltpu.VMEM((ch, cells), BF16), pltpu.VMEM((ch, cells), BF16),
            pltpu.VMEM((cells, ch), F32), pltpu.VMEM((cells, ch), F32), pltpu.VMEM((cells, ch), BF16),
            pltpu.VMEM((4, 8, rows, ch), F32), pltpu.VMEM((4, 8, rows, ch), F32),
            pltpu.VMEM((4, 2, cols, ch), BF16), pltpu.VMEM((4, 2, cols, ch), BF16),
            pltpu.VMEM((6, 6 * ch, lanes), F32), pltpu.VMEM((6, half, lanes), F32),
            pltpu.VMEM((6, half, lanes), BF16), pltpu.VMEM((6, half, lanes), F32), pltpu.VMEM((6, half, lanes), BF16),
            pltpu.VMEM((6, half // 2, lanes), BF16), pltpu.VMEM((6, half // 2, lanes), F32),
            pltpu.VMEM((6, half // 2, lanes), BF16),
            pltpu.VMEM((6, piece, lanes), F32), pltpu.VMEM((6, n_lon - 1, strip, lanes), F32),
            pltpu.VMEM((6, n_lon, piece, lanes), BF16), pltpu.VMEM((6, 6 * ch, lanes), BF16),
            pltpu.SemaphoreType.DMA((4, 8)), pltpu.SemaphoreType.DMA((4, 8)),
            pltpu.SemaphoreType.DMA((6, copies)), pltpu.SemaphoreType.DMA((6, copies)),
        ],
        compiler_params=pltpu.CompilerParams(
            collective_id=0, has_side_effects=True, vmem_limit_bytes=52 * 1024 * 1024
        ),
        cost_estimate=pl.CostEstimate(
            flops=12 * 9 * ch * ch * cells, bytes_accessed=8 * 9 * ch * ch, transcendentals=2 * cells * ch
        ),
    )(by_cells(fields), by_cells(cotangent), weight_one, weight_two, edge_flips)

    def by_channels(array):
        return jnp.transpose(array.reshape(rows, cols, ch), (2, 0, 1))[None]

    return (
        by_channels(out),
        by_channels(grad_fields),
        grad_one.astype(F32),
        grad_two.astype(F32),
    )


def solution(mesh):
    tile = P("dp", None, "lat", "lon")
    sizes = tuple(mesh.shape[axis] for axis in ("lon", "lat", "dp"))
    return jax.shard_map(
        functools.partial(per_device, sizes), mesh=mesh,
        in_specs=(tile, P(), P(), P(), tile), out_specs=(tile, tile, P(), P()), check_vma=False,
    )
```

```python
import functools

import jax
import jax.numpy as jnp
from jax import lax
from jax.experimental import pallas as pl
from jax.experimental.pallas import tpu as pltpu
from jax.sharding import PartitionSpec as P

F32 = jnp.float32
BF16 = jnp.bfloat16
NN = (((1,), (0,)), ((), ()))
NT = (((1,), (1,)), ((), ()))
SIDES = ("W", "E", "U", "D", "UW", "UE", "DW", "DE")


def product(a, b, dims):
    return lax.dot_general(a, b, dims, preferred_element_type=F32)


def kernel(
    sizes,
    x_ref, g_ref, w1_ref, w2_ref, flip_ref,
    out_ref, gf_ref, o1_ref, o2_ref,
    x1, x2, gz, bz, gt, bt, q, hid, act,
    cell_out, cell_in, row_out, row_in,
    a0, r0, s1, a1, r1, a3, r3, near, full,
    halo_send, halo_recv, sum_send, sum_recv,
):
    n_lon, n_lat, n_dp, rows, cols, ch = sizes
    cells = rows * cols
    ny = n_dp // 2
    lon, lat, dp = lax.axis_index("lon"), lax.axis_index("lat"), lax.axis_index("dp")
    core, y = lax.rem(dp, 2), lax.div(dp, 2)
    west, east = lax.rem(lon + n_lon - 1, n_lon), lax.rem(lon + 1, n_lon)
    has_up, has_down = lat > 0, lat < n_lat - 1
    up, down = jnp.maximum(lat - 1, 0), jnp.minimum(lat + 1, n_lat - 1)

    cell_in[...] = jnp.zeros_like(cell_in)
    cell_out[...] = jnp.zeros_like(cell_out)
    row_in[...] = jnp.zeros_like(row_in)
    barrier = pltpu.get_barrier_semaphore()
    greeted = 0
    for i in range(n_lon):
        for j in range(n_lat):
            if i or j:
                pl.semaphore_signal(
                    barrier, inc=1,
                    device_id={"lon": lax.rem(lon + i, n_lon), "lat": lax.rem(lat + j, n_lat), "dp": dp},
                    device_id_type=pl.DeviceIdType.MESH,
                )
                greeted += 1
    for k in range(1, n_dp):
        pl.semaphore_signal(
            barrier, inc=1,
            device_id={"lon": lon, "lat": lat, "dp": lax.rem(dp + k, n_dp)},
            device_id_type=pl.DeviceIdType.MESH,
        )
        greeted += 1

    for k in range(1, ny):
        for j in range(1, n_lat):
            pl.semaphore_signal(
                barrier, inc=1,
                device_id={
                    "lon": lon, "lat": lax.rem(lat + j, n_lat), "dp": lax.rem(y + k, ny) * 2 + core,
                },
                device_id_type=pl.DeviceIdType.MESH,
            )
            greeted += 1

    def remote(src, dst, send, recv, to_lon, to_lat, to_dp):
        return pltpu.make_async_remote_copy(
            src_ref=src, dst_ref=dst, send_sem=send, recv_sem=recv,
            device_id={"lon": to_lon, "lat": to_lat, "dp": to_dp},
            device_id_type=pl.DeviceIdType.MESH,
        )

    opposite = {"W": "E", "E": "W", "U": "D", "D": "U", "UW": "DE", "UE": "DW", "DW": "UE", "DE": "UW"}

    def halo_copy(e, side):
        to_lon = west if "W" in side else east if "E" in side else lon
        to_lat = up if "U" in side else down if "D" in side else lat
        slot, there = SIDES.index(side), SIDES.index(opposite[side])
        if side in ("U", "D"):
            src, dst = row_out.at[e, slot - 2], row_in.at[e, there - 2]
        else:
            src, dst = cell_out.at[e, slot], cell_in.at[e, there]
        return remote(src, dst, halo_send.at[e, slot], halo_recv.at[e, there], to_lon, to_lat, dp)

    def guarded(side, action):
        if "U" in side:
            pl.when(has_up)(action)
        elif "D" in side:
            pl.when(has_down)(action)
        else:
            action()

    def halo_start(e):
        for side in ("U", "D", "W", "E", "UW", "UE", "DW", "DE"):
            copy = halo_copy(e, side)
            guarded(side, copy.start)

    def halo_wait(e):
        for side in SIDES:
            copy = halo_copy(e, side)
            guarded(side, copy.wait_send)
            guarded(opposite[side], copy.wait_recv)

    line = lax.broadcasted_iota(jnp.int32, (cols, ch), 0)
    ja = lax.broadcasted_iota(jnp.int32, (cols, cols), 0)
    jb = lax.broadcasted_iota(jnp.int32, (cols, cols), 1)
    exchange = jnp.where(ja + jb == cols - 1, 1.0, 0.0).astype(BF16)
    zero = jnp.zeros((1, ch), jnp.int32)
    flip_up = zero + flip_ref[jnp.maximum(lat - 1, 0), lon] == 1
    flip_down = zero + flip_ref[jnp.minimum(lat, n_lat - 2), lon] == 1

    def turned(flag, west_cell, middle, east_cell):
        back = product(exchange, middle, NN)
        return (
            jnp.where(flag, east_cell, west_cell),
            jnp.where(flag, back, middle.astype(F32)),
            jnp.where(flag, west_cell, east_cell),
        )

    def send_field(e, ref):
        for h in range(rows):
            top = ref[h * cols : h * cols + 16, :].astype(F32)
            low = ref[(h + 1) * cols - 16 : (h + 1) * cols, :].astype(F32)
            cell_out[e, 0, h : h + 1, :] = top[0:1]
            cell_out[e, 1, h : h + 1, :] = low[15:16]
            if h == 0:
                cell_out[e, 4, 0:1, :] = top[0:1]
                cell_out[e, 5, 0:1, :] = low[15:16]
            if h == rows - 1:
                cell_out[e, 6, 0:1, :] = top[0:1]
                cell_out[e, 7, 0:1, :] = low[15:16]
        row_out[e, 0] = ref[0:cols, :]
        row_out[e, 1] = ref[cells - cols : cells, :]
        halo_start(e)

    def put_row(buf, i, west_cell, middle, east_cell):
        at = slice(i * cols, (i + 1) * cols)
        buf[at, 0:ch] = jnp.where(line == 0, west_cell, pltpu.roll(middle, 1, 0)).astype(BF16)
        buf[at, ch : 2 * ch] = middle.astype(BF16)
        buf[at, 2 * ch : 3 * ch] = jnp.where(
            line == cols - 1, east_cell, pltpu.roll(middle, cols - 1, 0)
        ).astype(BF16)

    def pad_field(e, ref, buf):
        halo_wait(e)
        for h in range(rows):
            put_row(
                buf, h + 1, cell_in[e, 0, h : h + 1, :],
                ref[h * cols : (h + 1) * cols, :].astype(F32), cell_in[e, 1, h : h + 1, :],
            )
        put_row(buf, 0, *turned(flip_up, cell_in[e, 4, 0:1, :], row_in[e, 0], cell_in[e, 5, 0:1, :]))
        put_row(buf, rows + 1, *turned(flip_down, cell_in[e, 6, 0:1, :], row_in[e, 1], cell_in[e, 7, 0:1, :]))

    block = cells // 2

    def conv(buf, w_ref, i):
        left = jnp.concatenate(
            [buf[i * block + r * cols : i * block + r * cols + block, :] for r in range(3)], 1
        )
        right = jnp.concatenate([w_ref[t] for t in range(9)], 1)
        return product(left, right, NT)

    def back_conv(e, z, w_ref):
        step = (rows + 2) // 2
        size = step * cols
        for i in range(2):
            left = jnp.concatenate(
                [z[i * size + (2 - r) * cols : i * size + (2 - r) * cols + size, :] for r in range(3)], 1
            )
            ys = [
                product(left, jnp.concatenate([w_ref[3 * r + s] for r in range(3)], 0), NN)
                for s in range(3)
            ]
            for k in range(step):
                n = i * step + k
                at = slice(k * cols, (k + 1) * cols)
                y0, y1, y2 = ys[0][at], ys[1][at], ys[2][at]
                total = (
                    y1
                    + jnp.where(line == cols - 1, 0.0, pltpu.roll(y0, cols - 1, 0))
                    + jnp.where(line == 0, 0.0, pltpu.roll(y2, 1, 0))
                )
                if 0 < n < rows + 1:
                    q[(n - 1) * cols : n * cols, :] = total
                    cell_out[e, 0, n - 1 : n, :] = y0[0:1]
                    cell_out[e, 1, n - 1 : n, :] = y2[cols - 1 : cols]
                else:
                    flag, slot = (flip_up, 0) if n == 0 else (flip_down, 1)
                    first, middle, last = turned(
                        flag, y0[0:1], total.astype(BF16), y2[cols - 1 : cols]
                    )
                    row_out[e, slot] = middle.astype(BF16)
                    cell_out[e, 4 + 2 * slot, 0:1, :] = first
                    cell_out[e, 5 + 2 * slot, 0:1, :] = last
            tick()
        halo_start(e)

    def returned_row(e, h):
        value = q[h * cols : (h + 1) * cols, :]
        west_cell, east_cell = cell_in[e, 0, h : h + 1, :], cell_in[e, 1, h : h + 1, :]
        if h == 0:
            value = value + row_in[e, 0].astype(F32)
            west_cell = west_cell + cell_in[e, 4, 0:1, :]
            east_cell = east_cell + cell_in[e, 5, 0:1, :]
        if h == rows - 1:
            value = value + row_in[e, 1].astype(F32)
            west_cell = west_cell + cell_in[e, 6, 0:1, :]
            east_cell = east_cell + cell_in[e, 7, 0:1, :]
        return value + jnp.where(line == 0, west_cell, 0.0) + jnp.where(line == cols - 1, east_cell, 0.0)

    lanes = ch // 2
    part_rows = 6 * ch
    half = part_rows // 2
    piece = half // (ny * n_lat)
    strip = piece // n_lon
    scattered = strip % 16 == 0

    def rows_of(start, size):
        return pl.ds(pl.multiple_of(start, 16), size)

    plane = ny * n_lat

    def plane_place(k):
        return lax.rem(y + k // n_lat, ny) * n_lat + lax.rem(lat + k % n_lat, n_lat)

    def reduce_steps(p, grad):
        target = full.at[p]
        sem = iter(range(1000))

        def send(src, dst, axis, k=1):
            slot = next(sem)
            to = {"lon": lon, "lat": lat, "dp": dp}
            if axis == "core":
                to["dp"] = y * 2 + 1 - core
            elif axis == "plane":
                to["dp"] = lax.rem(y + k // n_lat, ny) * 2 + core
                to["lat"] = lax.rem(lat + k % n_lat, n_lat)
            else:
                to["lon"] = lax.rem(lon + k, n_lon)
            copy = remote(
                src, dst, sum_send.at[p, slot], sum_recv.at[p, slot], to["lon"], to["lat"], to["dp"]
            )
            copy.start()
            return copy

        def finish(copies):
            for copy in copies:
                copy.wait()

        for n in range(6):
            a0[p, n * ch : (n + 1) * ch, :] = grad[:, n * lanes : (n + 1) * lanes]
        copies = [send(a0.at[p, rows_of((1 - core) * half, half), :], r0.at[p], "core")]
        yield
        finish(copies)
        total = a0[p, rows_of(core * half, half), :] + r0[p]
        a1[p] = total
        s1[p] = total.astype(BF16)
        copies = []
        for k in range(1, plane):
            there = rows_of(plane_place(k) * piece, piece)
            copies.append(send(s1.at[p, there, :], r1.at[p, (k - 1) * piece : k * piece, :], "plane", k))
        yield
        finish(copies)
        total = a1[p, rows_of(plane_place(0) * piece, piece), :]
        for k in range(1, plane):
            total = total + r1[p, (k - 1) * piece : k * piece, :].astype(F32)
        at2 = core * half + plane_place(0) * piece
        if scattered:
            a3[p] = total
            copies = []
            for k in range(1, n_lon):
                there = rows_of(lax.rem(lon + k, n_lon) * strip, strip)
                copies.append(send(a3.at[p, there, :], r3.at[p, k - 1], "lon", k))
            yield
            finish(copies)
            total = a3[p, rows_of(lon * strip, strip), :]
            for k in range(1, n_lon):
                total = total + r3[p, k - 1]
            own = target.at[rows_of(at2 + lon * strip, strip), :]
            own[...] = total.astype(BF16)
            copies = [send(own, own, "lon", k) for k in range(1, n_lon)]
            yield
            finish(copies)
        else:
            near[p, lon] = total.astype(BF16)
            copies = [send(near.at[p, lon], near.at[p, lon], "lon", k) for k in range(1, n_lon)]
            yield
            finish(copies)
            total = near[p, 0].astype(F32)
            for k in range(1, n_lon):
                total = total + near[p, k].astype(F32)
            target[rows_of(at2, piece), :] = total.astype(BF16)
        own = target.at[rows_of(at2, piece), :]
        copies = [send(own, own, "plane", k) for k in range(1, plane)]
        yield
        finish(copies)
        own = target.at[rows_of(core * half, half), :]
        copies = [send(own, own, "core")]
        yield
        finish(copies)
        result = o1_ref if p < 3 else o2_ref
        for n in range(6):
            result[3 * (p % 3) + n // 2, :, (n % 2) * lanes : (n % 2 + 1) * lanes] = full[
                p, n * ch : (n + 1) * ch, :
            ]

    patience = (2, 3, 2, 2, 3, 1)
    running = []

    def tick():
        for state in list(running):
            state["age"] += 1
            if state["age"] >= patience[state["step"]]:
                state["age"], state["step"] = 0, state["step"] + 1
                if next(state["steps"], "end") == "end":
                    running.remove(state)

    def begin(p, grad):
        steps = reduce_steps(p, grad)
        next(steps)
        tick()
        running.append({"steps": steps, "age": 0, "step": 0})

    edge = jnp.zeros((2 * cols, ch), BF16)
    for z in (gz, bz):
        z[0 : 2 * cols, :] = edge
        z[2 * cols + cells : 4 * cols + cells, :] = edge
    for h in range(rows):
        value = g_ref[h * cols : (h + 1) * cols, :]
        gz[(h + 2) * cols : (h + 3) * cols, :] = value
        gt[:, h * cols : (h + 1) * cols] = value.astype(F32).T.astype(BF16)
    pl.semaphore_wait(barrier, greeted)
    send_field(0, x_ref)
    back_conv(2, gz, w2_ref)

    pad_field(0, x_ref, x1)
    for i in range(2):
        value = conv(x1, w1_ref, i)
        hid[i * block : (i + 1) * block, :] = value
        act[i * block : (i + 1) * block, :] = (value / (1.0 + jnp.exp(-value))).astype(BF16)
    send_field(1, act)

    halo_wait(2)
    for h in range(rows):
        back = returned_row(2, h)
        value = hid[h * cols : (h + 1) * cols, :]
        sigma = 1.0 / (1.0 + jnp.exp(-value))
        back = back * sigma * (1.0 + value * (1.0 - sigma))
        bz[(h + 2) * cols : (h + 3) * cols, :] = back.astype(BF16)
        bt[:, h * cols : (h + 1) * cols] = back.T.astype(BF16)

    for r in range(3):
        begin(r, product(bt[...], x1[r * cols : r * cols + cells, :], NN))
    pad_field(1, act, x2)
    tick()
    for r in range(3):
        begin(3 + r, product(gt[...], x2[r * cols : r * cols + cells, :], NN))
    back_conv(3, bz, w1_ref)
    for i in range(2):
        at = slice(i * block, (i + 1) * block)
        out_ref[at, :] = (x_ref[at, :].astype(F32) + conv(x2, w2_ref, i)).astype(BF16)
        tick()
    halo_wait(3)
    for h in range(rows):
        at = slice(h * cols, (h + 1) * cols)
        gf_ref[at, :] = (g_ref[at, :].astype(F32) + returned_row(3, h)).astype(BF16)
    patience = (1,) * 8
    while running:
        tick()


def per_device(sizes, fields, weight_one, weight_two, edge_flips, cotangent):
    n_lon, n_lat, n_dp = sizes
    _, ch, rows, cols = fields.shape
    cells = rows * cols
    ny = n_dp // 2
    def by_cells(array):
        return jnp.transpose(array[0], (1, 2, 0)).reshape(cells, ch)

    part, half, lanes = 3 * ch, 3 * ch, ch // 2
    piece = half // (ny * n_lat)
    strip = max(8, piece // n_lon)
    copies = 2 * (ny * n_lat + n_lon)
    vmem = pl.BlockSpec(memory_space=pltpu.VMEM)
    padded = ((rows + 2) * cols, part)
    zeroed = ((rows + 4) * cols, ch)
    out, grad_fields, grad_one, grad_two = pl.pallas_call(
        functools.partial(kernel, (n_lon, n_lat, n_dp, rows, cols, ch)),
        out_shape=[jax.ShapeDtypeStruct((cells, ch), BF16)] * 2
        + [jax.ShapeDtypeStruct((9, ch, ch), BF16)] * 2,
        in_specs=[vmem] * 4 + [pl.BlockSpec(memory_space=pltpu.SMEM)],
        out_specs=[vmem] * 4,
        scratch_shapes=[
            pltpu.VMEM(padded, BF16), pltpu.VMEM(padded, BF16),
            pltpu.VMEM(zeroed, BF16), pltpu.VMEM(zeroed, BF16),
            pltpu.VMEM((ch, cells), BF16), pltpu.VMEM((ch, cells), BF16),
            pltpu.VMEM((cells, ch), F32), pltpu.VMEM((cells, ch), F32), pltpu.VMEM((cells, ch), BF16),
            pltpu.VMEM((4, 8, rows, ch), F32), pltpu.VMEM((4, 8, rows, ch), F32),
            pltpu.VMEM((4, 2, cols, ch), BF16), pltpu.VMEM((4, 2, cols, ch), BF16),
            pltpu.VMEM((6, 6 * ch, lanes), F32), pltpu.VMEM((6, half, lanes), F32),
            pltpu.VMEM((6, half, lanes), BF16), pltpu.VMEM((6, half, lanes), F32), pltpu.VMEM((6, half, lanes), BF16),
            pltpu.VMEM((6, piece, lanes), F32), pltpu.VMEM((6, n_lon - 1, strip, lanes), F32),
            pltpu.VMEM((6, n_lon, piece, lanes), BF16), pltpu.VMEM((6, 6 * ch, lanes), BF16),
            pltpu.SemaphoreType.DMA((4, 8)), pltpu.SemaphoreType.DMA((4, 8)),
            pltpu.SemaphoreType.DMA((6, copies)), pltpu.SemaphoreType.DMA((6, copies)),
        ],
        compiler_params=pltpu.CompilerParams(
            collective_id=0, has_side_effects=True, vmem_limit_bytes=52 * 1024 * 1024
        ),
        cost_estimate=pl.CostEstimate(
            flops=12 * 9 * ch * ch * cells, bytes_accessed=8 * 9 * ch * ch, transcendentals=2 * cells * ch
        ),
    )(by_cells(fields), by_cells(cotangent), weight_one, weight_two, edge_flips)

    def by_channels(array):
        return jnp.transpose(array.reshape(rows, cols, ch), (2, 0, 1))[None]

    return (
        by_channels(out),
        by_channels(grad_fields),
        grad_one.astype(F32),
        grad_two.astype(F32),
    )


def solution(mesh):
    tile = P("dp", None, "lat", "lon")
    sizes = tuple(mesh.shape[axis] for axis in ("lon", "lat", "dp"))
    return jax.shard_map(
        functools.partial(per_device, sizes), mesh=mesh,
        in_specs=(tile, P(), P(), P(), tile), out_specs=(tile, tile, P(), P()), check_vma=False,
    )
```

```python
import functools

import jax
import jax.numpy as jnp
from jax import lax
from jax.experimental import pallas as pl
from jax.experimental.pallas import tpu as pltpu
from jax.sharding import PartitionSpec as P

F32 = jnp.float32
BF16 = jnp.bfloat16
NN = (((1,), (0,)), ((), ()))
NT = (((1,), (1,)), ((), ()))
SIDES = ("W", "E", "U", "D", "UW", "UE", "DW", "DE")


def product(a, b, dims):
    return lax.dot_general(a, b, dims, preferred_element_type=F32)


def kernel(
    sizes,
    x_ref, g_ref, w1_ref, w2_ref, flip_ref,
    out_ref, gf_ref, o1_ref, o2_ref,
    x1, x2, gz, bz, gt, bt, q, slope, act,
    cell_out, cell_in, row_out, row_in,
    a0, r0, s1, a1, r1, a3, r3, near, full,
    halo_send, halo_recv, sum_send, sum_recv,
):
    n_lon, n_lat, n_dp, rows, cols, ch = sizes
    cells = rows * cols
    ny = n_dp // 2
    lon, lat, dp = lax.axis_index("lon"), lax.axis_index("lat"), lax.axis_index("dp")
    core, y = lax.rem(dp, 2), lax.div(dp, 2)
    west, east = lax.rem(lon + n_lon - 1, n_lon), lax.rem(lon + 1, n_lon)
    has_up, has_down = lat > 0, lat < n_lat - 1
    up, down = jnp.maximum(lat - 1, 0), jnp.minimum(lat + 1, n_lat - 1)

    cell_in[...] = jnp.zeros_like(cell_in)
    cell_out[...] = jnp.zeros_like(cell_out)
    row_in[...] = jnp.zeros_like(row_in)
    barrier = pltpu.get_barrier_semaphore()
    greeted = 0
    for i in range(n_lon):
        for j in range(n_lat):
            if i or j:
                pl.semaphore_signal(
                    barrier, inc=1,
                    device_id={"lon": lax.rem(lon + i, n_lon), "lat": lax.rem(lat + j, n_lat), "dp": dp},
                    device_id_type=pl.DeviceIdType.MESH,
                )
                greeted += 1
    for k in range(1, n_dp):
        pl.semaphore_signal(
            barrier, inc=1,
            device_id={"lon": lon, "lat": lat, "dp": lax.rem(dp + k, n_dp)},
            device_id_type=pl.DeviceIdType.MESH,
        )
        greeted += 1

    for k in range(1, ny):
        for j in range(1, n_lat):
            pl.semaphore_signal(
                barrier, inc=1,
                device_id={
                    "lon": lon, "lat": lax.rem(lat + j, n_lat), "dp": lax.rem(y + k, ny) * 2 + core,
                },
                device_id_type=pl.DeviceIdType.MESH,
            )
            greeted += 1

    def remote(src, dst, send, recv, to_lon, to_lat, to_dp):
        return pltpu.make_async_remote_copy(
            src_ref=src, dst_ref=dst, send_sem=send, recv_sem=recv,
            device_id={"lon": to_lon, "lat": to_lat, "dp": to_dp},
            device_id_type=pl.DeviceIdType.MESH,
        )

    opposite = {"W": "E", "E": "W", "U": "D", "D": "U", "UW": "DE", "UE": "DW", "DW": "UE", "DE": "UW"}

    def halo_copy(e, side):
        to_lon = west if "W" in side else east if "E" in side else lon
        to_lat = up if "U" in side else down if "D" in side else lat
        slot, there = SIDES.index(side), SIDES.index(opposite[side])
        if side in ("U", "D"):
            src, dst = row_out.at[e, slot - 2], row_in.at[e, there - 2]
        else:
            src, dst = cell_out.at[e, slot], cell_in.at[e, there]
        return remote(src, dst, halo_send.at[e, slot], halo_recv.at[e, there], to_lon, to_lat, dp)

    def guarded(side, action):
        if "U" in side:
            pl.when(has_up)(action)
        elif "D" in side:
            pl.when(has_down)(action)
        else:
            action()

    def halo_start(e):
        for side in ("U", "D", "W", "E", "UW", "UE", "DW", "DE"):
            copy = halo_copy(e, side)
            guarded(side, copy.start)

    def halo_wait(e):
        for side in SIDES:
            copy = halo_copy(e, side)
            guarded(side, copy.wait_send)
            guarded(opposite[side], copy.wait_recv)

    line = lax.broadcasted_iota(jnp.int32, (cols, ch), 0)
    ja = lax.broadcasted_iota(jnp.int32, (cols, cols), 0)
    jb = lax.broadcasted_iota(jnp.int32, (cols, cols), 1)
    exchange = jnp.where(ja + jb == cols - 1, 1.0, 0.0).astype(BF16)
    zero = jnp.zeros((1, ch), jnp.int32)
    flip_up = zero + flip_ref[jnp.maximum(lat - 1, 0), lon] == 1
    flip_down = zero + flip_ref[jnp.minimum(lat, n_lat - 2), lon] == 1

    def turned(flag, west_cell, middle, east_cell):
        back = product(exchange, middle, NN)
        return (
            jnp.where(flag, east_cell, west_cell),
            jnp.where(flag, back, middle.astype(F32)),
            jnp.where(flag, west_cell, east_cell),
        )

    def send_field(e, ref):
        for h in range(rows):
            top = ref[h * cols : h * cols + 16, :].astype(F32)
            low = ref[(h + 1) * cols - 16 : (h + 1) * cols, :].astype(F32)
            cell_out[e, 0, h : h + 1, :] = top[0:1]
            cell_out[e, 1, h : h + 1, :] = low[15:16]
            if h == 0:
                cell_out[e, 4, 0:1, :] = top[0:1]
                cell_out[e, 5, 0:1, :] = low[15:16]
            if h == rows - 1:
                cell_out[e, 6, 0:1, :] = top[0:1]
                cell_out[e, 7, 0:1, :] = low[15:16]
        row_out[e, 0] = ref[0:cols, :]
        row_out[e, 1] = ref[cells - cols : cells, :]
        halo_start(e)

    def put_row(buf, i, west_cell, middle, east_cell):
        at = slice(i * cols, (i + 1) * cols)
        buf[at, 0:ch] = jnp.where(line == 0, west_cell, pltpu.roll(middle, 1, 0)).astype(BF16)
        buf[at, ch : 2 * ch] = middle.astype(BF16)
        buf[at, 2 * ch : 3 * ch] = jnp.where(
            line == cols - 1, east_cell, pltpu.roll(middle, cols - 1, 0)
        ).astype(BF16)

    def pad_field(e, ref, buf):
        halo_wait(e)
        for h in range(rows):
            put_row(
                buf, h + 1, cell_in[e, 0, h : h + 1, :],
                ref[h * cols : (h + 1) * cols, :].astype(F32), cell_in[e, 1, h : h + 1, :],
            )
        put_row(buf, 0, *turned(flip_up, cell_in[e, 4, 0:1, :], row_in[e, 0], cell_in[e, 5, 0:1, :]))
        put_row(buf, rows + 1, *turned(flip_down, cell_in[e, 6, 0:1, :], row_in[e, 1], cell_in[e, 7, 0:1, :]))

    block = cells // 2

    def conv(buf, w_ref, i):
        left = jnp.concatenate(
            [buf[i * block + r * cols : i * block + r * cols + block, :] for r in range(3)], 1
        )
        right = jnp.concatenate([w_ref[t] for t in range(9)], 1)
        return product(left, right, NT)

    def back_conv(e, z, w_ref, after=((), ())):
        step = (rows + 2) // 2
        size = step * cols
        for i in range(2):
            left = jnp.concatenate(
                [z[i * size + (2 - r) * cols : i * size + (2 - r) * cols + size, :] for r in range(3)], 1
            )
            ys = [
                product(left, jnp.concatenate([w_ref[3 * r + s] for r in range(3)], 0), NN)
                for s in range(3)
            ]
            for k in range(step):
                n = i * step + k
                at = slice(k * cols, (k + 1) * cols)
                y0, y1, y2 = ys[0][at], ys[1][at], ys[2][at]
                total = (
                    y1
                    + jnp.where(line == cols - 1, 0.0, pltpu.roll(y0, cols - 1, 0))
                    + jnp.where(line == 0, 0.0, pltpu.roll(y2, 1, 0))
                )
                if 0 < n < rows + 1:
                    q[(n - 1) * cols : n * cols, :] = total
                    cell_out[e, 0, n - 1 : n, :] = y0[0:1]
                    cell_out[e, 1, n - 1 : n, :] = y2[cols - 1 : cols]
                else:
                    flag, slot = (flip_up, 0) if n == 0 else (flip_down, 1)
                    first, middle, last = turned(
                        flag, y0[0:1], total.astype(BF16), y2[cols - 1 : cols]
                    )
                    row_out[e, slot] = middle.astype(BF16)
                    cell_out[e, 4 + 2 * slot, 0:1, :] = first
                    cell_out[e, 5 + 2 * slot, 0:1, :] = last
            advance(*after[i])
        halo_start(e)

    def returned_row(e, h):
        value = q[h * cols : (h + 1) * cols, :]
        west_cell, east_cell = cell_in[e, 0, h : h + 1, :], cell_in[e, 1, h : h + 1, :]
        if h == 0:
            value = value + row_in[e, 0].astype(F32)
            west_cell = west_cell + cell_in[e, 4, 0:1, :]
            east_cell = east_cell + cell_in[e, 5, 0:1, :]
        if h == rows - 1:
            value = value + row_in[e, 1].astype(F32)
            west_cell = west_cell + cell_in[e, 6, 0:1, :]
            east_cell = east_cell + cell_in[e, 7, 0:1, :]
        return value + jnp.where(line == 0, west_cell, 0.0) + jnp.where(line == cols - 1, east_cell, 0.0)

    lanes = ch // 2
    part_rows = 6 * ch
    half = part_rows // 2
    piece = half // (ny * n_lat)
    strip = piece // n_lon
    scattered = strip % 16 == 0

    def rows_of(start, size):
        return pl.ds(pl.multiple_of(start, 16), size)

    plane = ny * n_lat

    def plane_place(k):
        return lax.rem(y + k // n_lat, ny) * n_lat + lax.rem(lat + k % n_lat, n_lat)

    def reduce_steps(p, grad):
        target = full.at[p]
        sem = iter(range(1000))

        def send(src, dst, axis, k=1):
            slot = next(sem)
            to = {"lon": lon, "lat": lat, "dp": dp}
            if axis == "core":
                to["dp"] = y * 2 + 1 - core
            elif axis == "plane":
                to["dp"] = lax.rem(y + k // n_lat, ny) * 2 + core
                to["lat"] = lax.rem(lat + k % n_lat, n_lat)
            else:
                to["lon"] = lax.rem(lon + k, n_lon)
            copy = remote(
                src, dst, sum_send.at[p, slot], sum_recv.at[p, slot], to["lon"], to["lat"], to["dp"]
            )
            copy.start()
            return copy

        def finish(copies):
            for copy in copies:
                copy.wait()

        for n in range(6):
            a0[p, n * ch : (n + 1) * ch, :] = grad[:, n * lanes : (n + 1) * lanes]
        copies = [send(a0.at[p, rows_of((1 - core) * half, half), :], r0.at[p], "core")]
        yield
        finish(copies)
        total = a0[p, rows_of(core * half, half), :] + r0[p]
        a1[p] = total
        s1[p] = total.astype(BF16)
        copies = []
        for k in range(1, plane):
            there = rows_of(plane_place(k) * piece, piece)
            copies.append(send(s1.at[p, there, :], r1.at[p, (k - 1) * piece : k * piece, :], "plane", k))
        yield
        finish(copies)
        total = a1[p, rows_of(plane_place(0) * piece, piece), :]
        for k in range(1, plane):
            total = total + r1[p, (k - 1) * piece : k * piece, :].astype(F32)
        at2 = core * half + plane_place(0) * piece
        if scattered:
            a3[p] = total
            copies = []
            for k in range(1, n_lon):
                there = rows_of(lax.rem(lon + k, n_lon) * strip, strip)
                copies.append(send(a3.at[p, there, :], r3.at[p, k - 1], "lon", k))
            yield
            finish(copies)
            total = a3[p, rows_of(lon * strip, strip), :]
            for k in range(1, n_lon):
                total = total + r3[p, k - 1]
            own = target.at[rows_of(at2 + lon * strip, strip), :]
            own[...] = total.astype(BF16)
            copies = [send(own, own, "lon", k) for k in range(1, n_lon)]
            yield
            finish(copies)
        else:
            near[p, lon] = total.astype(BF16)
            copies = [send(near.at[p, lon], near.at[p, lon], "lon", k) for k in range(1, n_lon)]
            yield
            finish(copies)
            total = near[p, 0].astype(F32)
            for k in range(1, n_lon):
                total = total + near[p, k].astype(F32)
            target[rows_of(at2, piece), :] = total.astype(BF16)
        own = target.at[rows_of(at2, piece), :]
        copies = [send(own, own, "plane", k) for k in range(1, plane)]
        yield
        finish(copies)
        own = target.at[rows_of(core * half, half), :]
        copies = [send(own, own, "core")]
        yield
        finish(copies)
        result = o1_ref if p < 3 else o2_ref
        for n in range(6):
            result[3 * (p % 3) + n // 2, :, (n % 2) * lanes : (n % 2 + 1) * lanes] = full[
                p, n * ch : (n + 1) * ch, :
            ]

    running = {}

    def advance(*parts):
        for p in parts:
            if p in running and next(running[p], "end") == "end":
                del running[p]

    def begin(p, grad):
        running[p] = reduce_steps(p, grad)
        next(running[p])

    edge = jnp.zeros((2 * cols, ch), BF16)
    for z in (gz, bz):
        z[0 : 2 * cols, :] = edge
        z[2 * cols + cells : 4 * cols + cells, :] = edge
    for h in range(rows):
        value = g_ref[h * cols : (h + 1) * cols, :]
        gz[(h + 2) * cols : (h + 3) * cols, :] = value
        gt[:, h * cols : (h + 1) * cols] = value.astype(F32).T.astype(BF16)
    pl.semaphore_wait(barrier, greeted)
    send_field(0, x_ref)
    back_conv(2, gz, w2_ref)

    pad_field(0, x_ref, x1)
    for i in range(2):
        at = slice(i * block, (i + 1) * block)
        value = conv(x1, w1_ref, i)
        sigma = 1.0 / (1.0 + jnp.exp(-value))
        act[at, :] = (value * sigma).astype(BF16)
        slope[at, :] = sigma * (1.0 + value * (1.0 - sigma))
    send_field(1, act)

    halo_wait(2)
    for h in range(rows):
        back = returned_row(2, h) * slope[h * cols : (h + 1) * cols, :]
        bz[(h + 2) * cols : (h + 3) * cols, :] = back.astype(BF16)
        bt[:, h * cols : (h + 1) * cols] = back.T.astype(BF16)

    for r, ready in enumerate(((), (), (0,))):
        begin(r, product(bt[...], x1[r * cols : r * cols + cells, :], NN))
        advance(*ready)
    pad_field(1, act, x2)
    advance(1)
    for r, ready in enumerate(((2,), (0,), (3,))):
        begin(3 + r, product(gt[...], x2[r * cols : r * cols + cells, :], NN))
        advance(*ready)
    back_conv(3, bz, w1_ref, ((4, 5, 1), (0, 2)))
    for i, ready in enumerate(((1, 3), (0, 2, 4))):
        at = slice(i * block, (i + 1) * block)
        out_ref[at, :] = (x_ref[at, :].astype(F32) + conv(x2, w2_ref, i)).astype(BF16)
        advance(*ready)
    halo_wait(3)
    for h in range(rows):
        at = slice(h * cols, (h + 1) * cols)
        gf_ref[at, :] = (g_ref[at, :].astype(F32) + returned_row(3, h)).astype(BF16)
    while running:
        advance(*sorted(running, reverse=True))


def per_device(sizes, fields, weight_one, weight_two, edge_flips, cotangent):
    n_lon, n_lat, n_dp = sizes
    _, ch, rows, cols = fields.shape
    cells = rows * cols
    ny = n_dp // 2
    def by_cells(array):
        return jnp.transpose(array[0], (1, 2, 0)).reshape(cells, ch)

    part, half, lanes = 3 * ch, 3 * ch, ch // 2
    piece = half // (ny * n_lat)
    strip = max(8, piece // n_lon)
    copies = 2 * (ny * n_lat + n_lon)
    vmem = pl.BlockSpec(memory_space=pltpu.VMEM)
    padded = ((rows + 2) * cols, part)
    zeroed = ((rows + 4) * cols, ch)
    out, grad_fields, grad_one, grad_two = pl.pallas_call(
        functools.partial(kernel, (n_lon, n_lat, n_dp, rows, cols, ch)),
        out_shape=[jax.ShapeDtypeStruct((cells, ch), BF16)] * 2
        + [jax.ShapeDtypeStruct((9, ch, ch), BF16)] * 2,
        in_specs=[vmem] * 4 + [pl.BlockSpec(memory_space=pltpu.SMEM)],
        out_specs=[vmem] * 4,
        scratch_shapes=[
            pltpu.VMEM(padded, BF16), pltpu.VMEM(padded, BF16),
            pltpu.VMEM(zeroed, BF16), pltpu.VMEM(zeroed, BF16),
            pltpu.VMEM((ch, cells), BF16), pltpu.VMEM((ch, cells), BF16),
            pltpu.VMEM((cells, ch), F32), pltpu.VMEM((cells, ch), F32), pltpu.VMEM((cells, ch), BF16),
            pltpu.VMEM((4, 8, rows, ch), F32), pltpu.VMEM((4, 8, rows, ch), F32),
            pltpu.VMEM((4, 2, cols, ch), BF16), pltpu.VMEM((4, 2, cols, ch), BF16),
            pltpu.VMEM((6, 6 * ch, lanes), F32), pltpu.VMEM((6, half, lanes), F32),
            pltpu.VMEM((6, half, lanes), BF16), pltpu.VMEM((6, half, lanes), F32), pltpu.VMEM((6, half, lanes), BF16),
            pltpu.VMEM((6, piece, lanes), F32), pltpu.VMEM((6, n_lon - 1, strip, lanes), F32),
            pltpu.VMEM((6, n_lon, piece, lanes), BF16), pltpu.VMEM((6, 6 * ch, lanes), BF16),
            pltpu.SemaphoreType.DMA((4, 8)), pltpu.SemaphoreType.DMA((4, 8)),
            pltpu.SemaphoreType.DMA((6, copies)), pltpu.SemaphoreType.DMA((6, copies)),
        ],
        compiler_params=pltpu.CompilerParams(
            collective_id=0, has_side_effects=True, vmem_limit_bytes=52 * 1024 * 1024
        ),
        cost_estimate=pl.CostEstimate(
            flops=12 * 9 * ch * ch * cells, bytes_accessed=8 * 9 * ch * ch, transcendentals=2 * cells * ch
        ),
    )(by_cells(fields), by_cells(cotangent), weight_one, weight_two, edge_flips)

    def by_channels(array):
        return jnp.transpose(array.reshape(rows, cols, ch), (2, 0, 1))[None]

    return (
        by_channels(out),
        by_channels(grad_fields),
        grad_one.astype(F32),
        grad_two.astype(F32),
    )


def solution(mesh):
    tile = P("dp", None, "lat", "lon")
    sizes = tuple(mesh.shape[axis] for axis in ("lon", "lat", "dp"))
    return jax.shard_map(
        functools.partial(per_device, sizes), mesh=mesh,
        in_specs=(tile, P(), P(), P(), tile), out_specs=(tile, tile, P(), P()), check_vma=False,
    )
```

```python
import functools

import jax
import jax.numpy as jnp
from jax import lax
from jax.experimental import pallas as pl
from jax.experimental.pallas import tpu as pltpu
from jax.sharding import PartitionSpec as P

F32 = jnp.float32
BF16 = jnp.bfloat16
NN = (((1,), (0,)), ((), ()))
NT = (((1,), (1,)), ((), ()))
SIDES = ("W", "E", "U", "D", "UW", "UE", "DW", "DE")


def product(a, b, dims):
    return lax.dot_general(a, b, dims, preferred_element_type=F32)


def kernel(
    sizes,
    x_ref, g_ref, w1_ref, w2_ref, flip_ref,
    out_ref, gf_ref, o1_ref, o2_ref,
    x1, x2, gz, bz, gt, bt, q, slope, act,
    cell_out, cell_in, row_out, row_in,
    a0, r0, s1, a1, r1, s2, a2, r2, a3, r3, near, full,
    halo_send, halo_recv, sum_send, sum_recv,
):
    n_lon, n_lat, n_dp, rows, cols, ch = sizes
    cells = rows * cols
    ny = n_dp // 2
    lon, lat, dp = lax.axis_index("lon"), lax.axis_index("lat"), lax.axis_index("dp")
    core, y = lax.rem(dp, 2), lax.div(dp, 2)
    west, east = lax.rem(lon + n_lon - 1, n_lon), lax.rem(lon + 1, n_lon)
    has_up, has_down = lat > 0, lat < n_lat - 1
    up, down = jnp.maximum(lat - 1, 0), jnp.minimum(lat + 1, n_lat - 1)

    cell_in[...] = jnp.zeros_like(cell_in)
    cell_out[...] = jnp.zeros_like(cell_out)
    row_in[...] = jnp.zeros_like(row_in)
    barrier = pltpu.get_barrier_semaphore()
    greeted = 0
    for i in range(n_lon):
        for j in range(n_lat):
            if i or j:
                pl.semaphore_signal(
                    barrier, inc=1,
                    device_id={"lon": lax.rem(lon + i, n_lon), "lat": lax.rem(lat + j, n_lat), "dp": dp},
                    device_id_type=pl.DeviceIdType.MESH,
                )
                greeted += 1
    for k in range(1, n_dp):
        pl.semaphore_signal(
            barrier, inc=1,
            device_id={"lon": lon, "lat": lat, "dp": lax.rem(dp + k, n_dp)},
            device_id_type=pl.DeviceIdType.MESH,
        )
        greeted += 1

    for k in range(1, ny):
        for j in range(1, n_lat):
            pl.semaphore_signal(
                barrier, inc=1,
                device_id={
                    "lon": lon, "lat": lax.rem(lat + j, n_lat), "dp": lax.rem(y + k, ny) * 2 + core,
                },
                device_id_type=pl.DeviceIdType.MESH,
            )
            greeted += 1

    def remote(src, dst, send, recv, to_lon, to_lat, to_dp):
        return pltpu.make_async_remote_copy(
            src_ref=src, dst_ref=dst, send_sem=send, recv_sem=recv,
            device_id={"lon": to_lon, "lat": to_lat, "dp": to_dp},
            device_id_type=pl.DeviceIdType.MESH,
        )

    opposite = {"W": "E", "E": "W", "U": "D", "D": "U", "UW": "DE", "UE": "DW", "DW": "UE", "DE": "UW"}

    def halo_copy(e, side):
        to_lon = west if "W" in side else east if "E" in side else lon
        to_lat = up if "U" in side else down if "D" in side else lat
        slot, there = SIDES.index(side), SIDES.index(opposite[side])
        if side in ("U", "D"):
            src, dst = row_out.at[e, slot - 2], row_in.at[e, there - 2]
        else:
            src, dst = cell_out.at[e, slot], cell_in.at[e, there]
        return remote(src, dst, halo_send.at[e, slot], halo_recv.at[e, there], to_lon, to_lat, dp)

    def guarded(side, action):
        if "U" in side:
            pl.when(has_up)(action)
        elif "D" in side:
            pl.when(has_down)(action)
        else:
            action()

    def halo_start(e):
        for side in ("U", "D", "W", "E", "UW", "UE", "DW", "DE"):
            copy = halo_copy(e, side)
            guarded(side, copy.start)

    def halo_wait(e):
        for side in SIDES:
            copy = halo_copy(e, side)
            guarded(side, copy.wait_send)
            guarded(opposite[side], copy.wait_recv)

    line = lax.broadcasted_iota(jnp.int32, (cols, ch), 0)
    ja = lax.broadcasted_iota(jnp.int32, (cols, cols), 0)
    jb = lax.broadcasted_iota(jnp.int32, (cols, cols), 1)
    exchange = jnp.where(ja + jb == cols - 1, 1.0, 0.0).astype(BF16)
    zero = jnp.zeros((1, ch), jnp.int32)
    flip_up = zero + flip_ref[jnp.maximum(lat - 1, 0), lon] == 1
    flip_down = zero + flip_ref[jnp.minimum(lat, n_lat - 2), lon] == 1

    def turned(flag, west_cell, middle, east_cell):
        back = product(exchange, middle, NN)
        return (
            jnp.where(flag, east_cell, west_cell),
            jnp.where(flag, back, middle.astype(F32)),
            jnp.where(flag, west_cell, east_cell),
        )

    def send_field(e, ref):
        for h in range(rows):
            top = ref[h * cols : h * cols + 16, :].astype(F32)
            low = ref[(h + 1) * cols - 16 : (h + 1) * cols, :].astype(F32)
            cell_out[e, 0, h : h + 1, :] = top[0:1]
            cell_out[e, 1, h : h + 1, :] = low[15:16]
            if h == 0:
                cell_out[e, 4, 0:1, :] = top[0:1]
                cell_out[e, 5, 0:1, :] = low[15:16]
            if h == rows - 1:
                cell_out[e, 6, 0:1, :] = top[0:1]
                cell_out[e, 7, 0:1, :] = low[15:16]
        row_out[e, 0] = ref[0:cols, :]
        row_out[e, 1] = ref[cells - cols : cells, :]
        halo_start(e)

    def put_row(buf, i, west_cell, middle, east_cell):
        at = slice(i * cols, (i + 1) * cols)
        buf[at, 0:ch] = jnp.where(line == 0, west_cell, pltpu.roll(middle, 1, 0)).astype(BF16)
        buf[at, ch : 2 * ch] = middle.astype(BF16)
        buf[at, 2 * ch : 3 * ch] = jnp.where(
            line == cols - 1, east_cell, pltpu.roll(middle, cols - 1, 0)
        ).astype(BF16)

    def pad_field(e, ref, buf):
        halo_wait(e)
        for h in range(rows):
            put_row(
                buf, h + 1, cell_in[e, 0, h : h + 1, :],
                ref[h * cols : (h + 1) * cols, :].astype(F32), cell_in[e, 1, h : h + 1, :],
            )
        put_row(buf, 0, *turned(flip_up, cell_in[e, 4, 0:1, :], row_in[e, 0], cell_in[e, 5, 0:1, :]))
        put_row(buf, rows + 1, *turned(flip_down, cell_in[e, 6, 0:1, :], row_in[e, 1], cell_in[e, 7, 0:1, :]))

    block = cells // 2

    def conv(buf, w_ref, i):
        left = jnp.concatenate(
            [buf[i * block + r * cols : i * block + r * cols + block, :] for r in range(3)], 1
        )
        right = jnp.concatenate([w_ref[t] for t in range(9)], 1)
        return product(left, right, NT)

    def back_conv(e, z, w_ref, halves=(0, 1), after=((), ())):
        step = (rows + 2) // 2
        size = step * cols
        for i in halves:
            left = jnp.concatenate(
                [z[i * size + (2 - r) * cols : i * size + (2 - r) * cols + size, :] for r in range(3)], 1
            )
            ys = [
                product(left, jnp.concatenate([w_ref[3 * r + s] for r in range(3)], 0), NN)
                for s in range(3)
            ]
            for k in range(step):
                n = i * step + k
                at = slice(k * cols, (k + 1) * cols)
                y0, y1, y2 = ys[0][at], ys[1][at], ys[2][at]
                total = (
                    y1
                    + jnp.where(line == cols - 1, 0.0, pltpu.roll(y0, cols - 1, 0))
                    + jnp.where(line == 0, 0.0, pltpu.roll(y2, 1, 0))
                )
                if 0 < n < rows + 1:
                    q[(n - 1) * cols : n * cols, :] = total
                    cell_out[e, 0, n - 1 : n, :] = y0[0:1]
                    cell_out[e, 1, n - 1 : n, :] = y2[cols - 1 : cols]
                else:
                    flag, slot = (flip_up, 0) if n == 0 else (flip_down, 1)
                    first, middle, last = turned(
                        flag, y0[0:1], total.astype(BF16), y2[cols - 1 : cols]
                    )
                    row_out[e, slot] = middle.astype(BF16)
                    cell_out[e, 4 + 2 * slot, 0:1, :] = first
                    cell_out[e, 5 + 2 * slot, 0:1, :] = last
            advance(*after[i])
        if 1 in halves:
            halo_start(e)

    def returned_row(e, h):
        value = q[h * cols : (h + 1) * cols, :]
        west_cell, east_cell = cell_in[e, 0, h : h + 1, :], cell_in[e, 1, h : h + 1, :]
        if h == 0:
            value = value + row_in[e, 0].astype(F32)
            west_cell = west_cell + cell_in[e, 4, 0:1, :]
            east_cell = east_cell + cell_in[e, 5, 0:1, :]
        if h == rows - 1:
            value = value + row_in[e, 1].astype(F32)
            west_cell = west_cell + cell_in[e, 6, 0:1, :]
            east_cell = east_cell + cell_in[e, 7, 0:1, :]
        return value + jnp.where(line == 0, west_cell, 0.0) + jnp.where(line == cols - 1, east_cell, 0.0)

    lanes = ch // 2
    part_rows = 6 * ch
    half = part_rows // 2
    piece = half // (ny * n_lat)
    strip = piece // n_lon
    scattered = strip % 16 == 0

    def rows_of(start, size):
        return pl.ds(pl.multiple_of(start, 16), size)

    plane = ny * n_lat

    def y_place(k):
        return lax.rem(y + k, ny)

    def lat_place(k):
        return lax.rem(lat + k, n_lat)

    def plane_place(k):
        return lax.rem(y + k // n_lat, ny) * n_lat + lax.rem(lat + k % n_lat, n_lat)

    def reduce_steps(p, grad):
        target = full.at[p]
        sem = iter(range(1000))

        def send(src, dst, axis, k=1):
            slot = next(sem)
            to = {"lon": lon, "lat": lat, "dp": dp}
            if axis == "core":
                to["dp"] = y * 2 + 1 - core
            elif axis == "y":
                to["dp"] = lax.rem(y + k, ny) * 2 + core
            elif axis == "lat":
                to["lat"] = lax.rem(lat + k, n_lat)
            elif axis == "plane":
                to["dp"] = lax.rem(y + k // n_lat, ny) * 2 + core
                to["lat"] = lax.rem(lat + k % n_lat, n_lat)
            else:
                to["lon"] = lax.rem(lon + k, n_lon)
            copy = remote(
                src, dst, sum_send.at[p, slot], sum_recv.at[p, slot], to["lon"], to["lat"], to["dp"]
            )
            copy.start()
            return copy

        def finish(copies):
            for copy in copies:
                copy.wait()

        for n in range(6):
            a0[p, n * ch : (n + 1) * ch, :] = grad[:, n * lanes : (n + 1) * lanes]
        copies = [send(a0.at[p, rows_of((1 - core) * half, half), :], r0.at[p], "core")]
        yield
        finish(copies)
        total = a0[p, rows_of(core * half, half), :] + r0[p]
        if p < 3:
            rounds = (("y", ny, y_place), ("lat", n_lat, lat_place))[:: 1 if p % 2 == 0 else -1]
        else:
            rounds = (("plane", plane, plane_place),)
        size, at2 = half, core * half
        trail = []
        for (axis, count, place), (kept, sent, got) in zip(rounds, ((a1, s1, r1), (a2, s2, r2))):
            kept[p, 0:size, :] = total
            sent[p, 0:size, :] = total.astype(BF16)
            size //= count
            copies = []
            for k in range(1, count):
                there = rows_of(place(k) * size, size)
                copies.append(send(sent.at[p, there, :], got.at[p, (k - 1) * size : k * size, :], axis, k))
            yield
            finish(copies)
            total = kept[p, rows_of(place(0) * size, size), :]
            for k in range(1, count):
                total = total + got[p, (k - 1) * size : k * size, :].astype(F32)
            at2 = at2 + place(0) * size
            trail.append((axis, count, at2, size))
        if scattered:
            a3[p] = total
            copies = []
            for k in range(1, n_lon):
                there = rows_of(lax.rem(lon + k, n_lon) * strip, strip)
                copies.append(send(a3.at[p, there, :], r3.at[p, k - 1], "lon", k))
            yield
            finish(copies)
            total = a3[p, rows_of(lon * strip, strip), :]
            for k in range(1, n_lon):
                total = total + r3[p, k - 1]
            own = target.at[rows_of(at2 + lon * strip, strip), :]
            own[...] = total.astype(BF16)
            copies = [send(own, own, "lon", k) for k in range(1, n_lon)]
            yield
            finish(copies)
        else:
            near[p, lon] = total.astype(BF16)
            copies = [send(near.at[p, lon], near.at[p, lon], "lon", k) for k in range(1, n_lon)]
            yield
            finish(copies)
            total = near[p, 0].astype(F32)
            for k in range(1, n_lon):
                total = total + near[p, k].astype(F32)
            target[rows_of(at2, piece), :] = total.astype(BF16)
        for axis, count, at, size in reversed(trail):
            own = target.at[rows_of(at, size), :]
            copies = [send(own, own, axis, k) for k in range(1, count)]
            yield
            finish(copies)
        own = target.at[rows_of(core * half, half), :]
        copies = [send(own, own, "core")]
        yield
        finish(copies)
        result = o2_ref if p < 3 else o1_ref
        for n in range(6):
            result[3 * (p % 3) + n // 2, :, (n % 2) * lanes : (n % 2 + 1) * lanes] = full[
                p, n * ch : (n + 1) * ch, :
            ]

    running = {}

    def advance(*parts):
        for p in parts:
            if p in running and next(running[p], "end") == "end":
                del running[p]

    def begin(p, grad):
        running[p] = reduce_steps(p, grad)
        next(running[p])

    edge = jnp.zeros((2 * cols, ch), BF16)
    for z in (gz, bz):
        z[0 : 2 * cols, :] = edge
        z[2 * cols + cells : 4 * cols + cells, :] = edge
    for h in range(rows):
        value = g_ref[h * cols : (h + 1) * cols, :]
        gz[(h + 2) * cols : (h + 3) * cols, :] = value
        gt[:, h * cols : (h + 1) * cols] = value.astype(F32).T.astype(BF16)
    pl.semaphore_wait(barrier, greeted)
    send_field(0, x_ref)
    back_conv(2, gz, w2_ref, (0,))

    pad_field(0, x_ref, x1)
    for i in range(2):
        at = slice(i * block, (i + 1) * block)
        value = conv(x1, w1_ref, i)
        sigma = 1.0 / (1.0 + jnp.exp(-value))
        act[at, :] = (value * sigma).astype(BF16)
        slope[at, :] = sigma * (1.0 + value * (1.0 - sigma))
    send_field(1, act)

    back_conv(2, gz, w2_ref, (1,))

    pad_field(1, act, x2)
    for r, ready in enumerate(((), (), (0,))):
        begin(r, product(gt[...], x2[r * cols : r * cols + cells, :], NN))
        advance(*ready)
    halo_wait(2)
    for h in range(rows):
        back = returned_row(2, h) * slope[h * cols : (h + 1) * cols, :]
        bz[(h + 2) * cols : (h + 3) * cols, :] = back.astype(BF16)
        bt[:, h * cols : (h + 1) * cols] = back.T.astype(BF16)
        if h == rows // 2:
            advance(1)
    advance(2)
    for r, ready in enumerate(((), (0, 1), (3, 2))):
        begin(3 + r, product(bt[...], x1[r * cols : r * cols + cells, :], NN))
        advance(*ready)
    back_conv(3, bz, w1_ref, after=((4, 5, 0), (3, 1, 2)))
    for i, ready in enumerate(((4, 0), (5, 1))):
        at = slice(i * block, (i + 1) * block)
        out_ref[at, :] = (x_ref[at, :].astype(F32) + conv(x2, w2_ref, i)).astype(BF16)
        advance(*ready)
    halo_wait(3)
    for h in range(rows):
        at = slice(h * cols, (h + 1) * cols)
        gf_ref[at, :] = (g_ref[at, :].astype(F32) + returned_row(3, h)).astype(BF16)
    advance(3, 2, 0)
    while running:
        advance(*sorted(running, reverse=True))


def per_device(sizes, fields, weight_one, weight_two, edge_flips, cotangent):
    n_lon, n_lat, n_dp = sizes
    _, ch, rows, cols = fields.shape
    cells = rows * cols
    ny = n_dp // 2
    def by_cells(array):
        return jnp.transpose(array[0], (1, 2, 0)).reshape(cells, ch)

    part, half, lanes = 3 * ch, 3 * ch, ch // 2
    piece = half // (ny * n_lat)
    strip = max(8, piece // n_lon)
    copies = 2 * (ny * n_lat + ny + n_lat + n_lon)
    vmem = pl.BlockSpec(memory_space=pltpu.VMEM)
    padded = ((rows + 2) * cols, part)
    zeroed = ((rows + 4) * cols, ch)
    out, grad_fields, grad_one, grad_two = pl.pallas_call(
        functools.partial(kernel, (n_lon, n_lat, n_dp, rows, cols, ch)),
        out_shape=[jax.ShapeDtypeStruct((cells, ch), BF16)] * 2
        + [jax.ShapeDtypeStruct((9, ch, ch), BF16)] * 2,
        in_specs=[vmem] * 4 + [pl.BlockSpec(memory_space=pltpu.SMEM)],
        out_specs=[vmem] * 4,
        scratch_shapes=[
            pltpu.VMEM(padded, BF16), pltpu.VMEM(padded, BF16),
            pltpu.VMEM(zeroed, BF16), pltpu.VMEM(zeroed, BF16),
            pltpu.VMEM((ch, cells), BF16), pltpu.VMEM((ch, cells), BF16),
            pltpu.VMEM((cells, ch), F32), pltpu.VMEM((cells, ch), F32), pltpu.VMEM((cells, ch), BF16),
            pltpu.VMEM((4, 8, rows, ch), F32), pltpu.VMEM((4, 8, rows, ch), F32),
            pltpu.VMEM((4, 2, cols, ch), BF16), pltpu.VMEM((4, 2, cols, ch), BF16),
            pltpu.VMEM((6, 6 * ch, lanes), F32), pltpu.VMEM((6, half, lanes), F32),
            pltpu.VMEM((6, half, lanes), BF16), pltpu.VMEM((6, half, lanes), F32), pltpu.VMEM((6, half, lanes), BF16),
            pltpu.VMEM((6, half // 2, lanes), BF16), pltpu.VMEM((6, half // 2, lanes), F32),
            pltpu.VMEM((6, half // 2, lanes), BF16),
            pltpu.VMEM((6, piece, lanes), F32), pltpu.VMEM((6, n_lon - 1, strip, lanes), F32),
            pltpu.VMEM((6, n_lon, piece, lanes), BF16), pltpu.VMEM((6, 6 * ch, lanes), BF16),
            pltpu.SemaphoreType.DMA((4, 8)), pltpu.SemaphoreType.DMA((4, 8)),
            pltpu.SemaphoreType.DMA((6, copies)), pltpu.SemaphoreType.DMA((6, copies)),
        ],
        compiler_params=pltpu.CompilerParams(
            collective_id=0, has_side_effects=True, vmem_limit_bytes=52 * 1024 * 1024
        ),
        cost_estimate=pl.CostEstimate(
            flops=12 * 9 * ch * ch * cells, bytes_accessed=8 * 9 * ch * ch, transcendentals=2 * cells * ch
        ),
    )(by_cells(fields), by_cells(cotangent), weight_one, weight_two, edge_flips)

    def by_channels(array):
        return jnp.transpose(array.reshape(rows, cols, ch), (2, 0, 1))[None]

    return (
        by_channels(out),
        by_channels(grad_fields),
        grad_one.astype(F32),
        grad_two.astype(F32),
    )


def solution(mesh):
    tile = P("dp", None, "lat", "lon")
    sizes = tuple(mesh.shape[axis] for axis in ("lon", "lat", "dp"))
    return jax.shard_map(
        functools.partial(per_device, sizes), mesh=mesh,
        in_specs=(tile, P(), P(), P(), tile), out_specs=(tile, tile, P(), P()), check_vma=False,
    )
```

```python
import functools

import jax
import jax.numpy as jnp
from jax import lax
from jax.experimental import pallas as pl
from jax.experimental.pallas import tpu as pltpu
from jax.sharding import PartitionSpec as P

F32 = jnp.float32
BF16 = jnp.bfloat16
NN = (((1,), (0,)), ((), ()))
NT = (((1,), (1,)), ((), ()))
SIDES = ("W", "E", "U", "D", "UW", "UE", "DW", "DE")


def product(a, b, dims):
    return lax.dot_general(a, b, dims, preferred_element_type=F32)


def kernel(
    sizes,
    x_ref, g_ref, w1_ref, w2_ref, flip_ref,
    out_ref, gf_ref, o1_ref, o2_ref,
    x1, x2, gz, bz, gt, bt, q, slope, act,
    cell_out, cell_in, row_out, row_in,
    a0, r0, s1, a1, r1, a3, r3, near, full,
    halo_send, halo_recv, sum_send, sum_recv,
):
    n_lon, n_lat, n_dp, rows, cols, ch = sizes
    cells = rows * cols
    ny = n_dp // 2
    lon, lat, dp = lax.axis_index("lon"), lax.axis_index("lat"), lax.axis_index("dp")
    core, y = lax.rem(dp, 2), lax.div(dp, 2)
    west, east = lax.rem(lon + n_lon - 1, n_lon), lax.rem(lon + 1, n_lon)
    has_up, has_down = lat > 0, lat < n_lat - 1
    up, down = jnp.maximum(lat - 1, 0), jnp.minimum(lat + 1, n_lat - 1)

    cell_in[...] = jnp.zeros_like(cell_in)
    cell_out[...] = jnp.zeros_like(cell_out)
    row_in[...] = jnp.zeros_like(row_in)
    barrier = pltpu.get_barrier_semaphore()
    greeted = 0
    for i in range(n_lon):
        for j in range(n_lat):
            if i or j:
                pl.semaphore_signal(
                    barrier, inc=1,
                    device_id={"lon": lax.rem(lon + i, n_lon), "lat": lax.rem(lat + j, n_lat), "dp": dp},
                    device_id_type=pl.DeviceIdType.MESH,
                )
                greeted += 1
    for k in range(1, n_dp):
        pl.semaphore_signal(
            barrier, inc=1,
            device_id={"lon": lon, "lat": lat, "dp": lax.rem(dp + k, n_dp)},
            device_id_type=pl.DeviceIdType.MESH,
        )
        greeted += 1

    for k in range(1, ny):
        for j in range(1, n_lat):
            pl.semaphore_signal(
                barrier, inc=1,
                device_id={
                    "lon": lon, "lat": lax.rem(lat + j, n_lat), "dp": lax.rem(y + k, ny) * 2 + core,
                },
                device_id_type=pl.DeviceIdType.MESH,
            )
            greeted += 1

    def remote(src, dst, send, recv, to_lon, to_lat, to_dp):
        return pltpu.make_async_remote_copy(
            src_ref=src, dst_ref=dst, send_sem=send, recv_sem=recv,
            device_id={"lon": to_lon, "lat": to_lat, "dp": to_dp},
            device_id_type=pl.DeviceIdType.MESH,
        )

    opposite = {"W": "E", "E": "W", "U": "D", "D": "U", "UW": "DE", "UE": "DW", "DW": "UE", "DE": "UW"}

    def halo_copy(e, side):
        to_lon = west if "W" in side else east if "E" in side else lon
        to_lat = up if "U" in side else down if "D" in side else lat
        slot, there = SIDES.index(side), SIDES.index(opposite[side])
        if side in ("U", "D"):
            src, dst = row_out.at[e, slot - 2], row_in.at[e, there - 2]
        else:
            src, dst = cell_out.at[e, slot], cell_in.at[e, there]
        return remote(src, dst, halo_send.at[e, slot], halo_recv.at[e, there], to_lon, to_lat, dp)

    def guarded(side, action):
        if "U" in side:
            pl.when(has_up)(action)
        elif "D" in side:
            pl.when(has_down)(action)
        else:
            action()

    def halo_start(e):
        for side in ("U", "D", "W", "E", "UW", "UE", "DW", "DE"):
            copy = halo_copy(e, side)
            guarded(side, copy.start)

    def halo_wait(e):
        for side in SIDES:
            copy = halo_copy(e, side)
            guarded(side, copy.wait_send)
            guarded(opposite[side], copy.wait_recv)

    line = lax.broadcasted_iota(jnp.int32, (cols, ch), 0)
    ja = lax.broadcasted_iota(jnp.int32, (cols, cols), 0)
    jb = lax.broadcasted_iota(jnp.int32, (cols, cols), 1)
    exchange = jnp.where(ja + jb == cols - 1, 1.0, 0.0).astype(BF16)
    zero = jnp.zeros((1, ch), jnp.int32)
    flip_up = zero + flip_ref[jnp.maximum(lat - 1, 0), lon] == 1
    flip_down = zero + flip_ref[jnp.minimum(lat, n_lat - 2), lon] == 1

    def turned(flag, west_cell, middle, east_cell):
        back = product(exchange, middle, NN)
        return (
            jnp.where(flag, east_cell, west_cell),
            jnp.where(flag, back, middle.astype(F32)),
            jnp.where(flag, west_cell, east_cell),
        )

    def send_field(e, ref):
        for h in range(rows):
            top = ref[h * cols : h * cols + 16, :].astype(F32)
            low = ref[(h + 1) * cols - 16 : (h + 1) * cols, :].astype(F32)
            cell_out[e, 0, h : h + 1, :] = top[0:1]
            cell_out[e, 1, h : h + 1, :] = low[15:16]
            if h == 0:
                cell_out[e, 4, 0:1, :] = top[0:1]
                cell_out[e, 5, 0:1, :] = low[15:16]
            if h == rows - 1:
                cell_out[e, 6, 0:1, :] = top[0:1]
                cell_out[e, 7, 0:1, :] = low[15:16]
        row_out[e, 0] = ref[0:cols, :]
        row_out[e, 1] = ref[cells - cols : cells, :]
        halo_start(e)

    def put_row(buf, i, west_cell, middle, east_cell):
        at = slice(i * cols, (i + 1) * cols)
        buf[at, 0:ch] = jnp.where(line == 0, west_cell, pltpu.roll(middle, 1, 0)).astype(BF16)
        buf[at, ch : 2 * ch] = middle.astype(BF16)
        buf[at, 2 * ch : 3 * ch] = jnp.where(
            line == cols - 1, east_cell, pltpu.roll(middle, cols - 1, 0)
        ).astype(BF16)

    def pad_field(e, ref, buf):
        halo_wait(e)
        for h in range(rows):
            put_row(
                buf, h + 1, cell_in[e, 0, h : h + 1, :],
                ref[h * cols : (h + 1) * cols, :].astype(F32), cell_in[e, 1, h : h + 1, :],
            )
        put_row(buf, 0, *turned(flip_up, cell_in[e, 4, 0:1, :], row_in[e, 0], cell_in[e, 5, 0:1, :]))
        put_row(buf, rows + 1, *turned(flip_down, cell_in[e, 6, 0:1, :], row_in[e, 1], cell_in[e, 7, 0:1, :]))

    block = cells // 2

    def conv(buf, w_ref, i):
        left = jnp.concatenate(
            [buf[i * block + r * cols : i * block + r * cols + block, :] for r in range(3)], 1
        )
        right = jnp.concatenate([w_ref[t] for t in range(9)], 1)
        return product(left, right, NT)

    def back_conv(e, z, w_ref, after=((), ())):
        step = (rows + 2) // 2
        size = step * cols
        for i in range(2):
            left = jnp.concatenate(
                [z[i * size + (2 - r) * cols : i * size + (2 - r) * cols + size, :] for r in range(3)], 1
            )
            ys = [
                product(left, jnp.concatenate([w_ref[3 * r + s] for r in range(3)], 0), NN)
                for s in range(3)
            ]
            for k in range(step):
                n = i * step + k
                at = slice(k * cols, (k + 1) * cols)
                y0, y1, y2 = ys[0][at], ys[1][at], ys[2][at]
                total = (
                    y1
                    + jnp.where(line == cols - 1, 0.0, pltpu.roll(y0, cols - 1, 0))
                    + jnp.where(line == 0, 0.0, pltpu.roll(y2, 1, 0))
                )
                if 0 < n < rows + 1:
                    q[(n - 1) * cols : n * cols, :] = total
                    cell_out[e, 0, n - 1 : n, :] = y0[0:1]
                    cell_out[e, 1, n - 1 : n, :] = y2[cols - 1 : cols]
                else:
                    flag, slot = (flip_up, 0) if n == 0 else (flip_down, 1)
                    first, middle, last = turned(
                        flag, y0[0:1], total.astype(BF16), y2[cols - 1 : cols]
                    )
                    row_out[e, slot] = middle.astype(BF16)
                    cell_out[e, 4 + 2 * slot, 0:1, :] = first
                    cell_out[e, 5 + 2 * slot, 0:1, :] = last
            advance(*after[i])
        halo_start(e)

    def returned_row(e, h):
        value = q[h * cols : (h + 1) * cols, :]
        west_cell, east_cell = cell_in[e, 0, h : h + 1, :], cell_in[e, 1, h : h + 1, :]
        if h == 0:
            value = value + row_in[e, 0].astype(F32)
            west_cell = west_cell + cell_in[e, 4, 0:1, :]
            east_cell = east_cell + cell_in[e, 5, 0:1, :]
        if h == rows - 1:
            value = value + row_in[e, 1].astype(F32)
            west_cell = west_cell + cell_in[e, 6, 0:1, :]
            east_cell = east_cell + cell_in[e, 7, 0:1, :]
        return value + jnp.where(line == 0, west_cell, 0.0) + jnp.where(line == cols - 1, east_cell, 0.0)

    lanes = ch // 2
    part_rows = 6 * ch
    half = part_rows // 2
    piece = half // (ny * n_lat)
    strip = piece // n_lon
    scattered = strip % 16 == 0

    def rows_of(start, size):
        return pl.ds(pl.multiple_of(start, 16), size)

    plane = ny * n_lat

    def plane_place(k):
        return lax.rem(y + k // n_lat, ny) * n_lat + lax.rem(lat + k % n_lat, n_lat)

    def reduce_steps(p, grad):
        target = full.at[p]
        sem = iter(range(1000))

        def send(src, dst, axis, k=1):
            slot = next(sem)
            to = {"lon": lon, "lat": lat, "dp": dp}
            if axis == "core":
                to["dp"] = y * 2 + 1 - core
            elif axis == "plane":
                to["dp"] = lax.rem(y + k // n_lat, ny) * 2 + core
                to["lat"] = lax.rem(lat + k % n_lat, n_lat)
            else:
                to["lon"] = lax.rem(lon + k, n_lon)
            copy = remote(
                src, dst, sum_send.at[p, slot], sum_recv.at[p, slot], to["lon"], to["lat"], to["dp"]
            )
            copy.start()
            return copy

        def finish(copies):
            for copy in copies:
                copy.wait()

        for n in range(6):
            a0[p, n * ch : (n + 1) * ch, :] = grad[:, n * lanes : (n + 1) * lanes]
        copies = [send(a0.at[p, rows_of((1 - core) * half, half), :], r0.at[p], "core")]
        yield
        finish(copies)
        total = a0[p, rows_of(core * half, half), :] + r0[p]
        a1[p] = total
        s1[p] = total.astype(BF16)
        copies = []
        for k in range(1, plane):
            there = rows_of(plane_place(k) * piece, piece)
            copies.append(send(s1.at[p, there, :], r1.at[p, (k - 1) * piece : k * piece, :], "plane", k))
        yield
        finish(copies)
        total = a1[p, rows_of(plane_place(0) * piece, piece), :]
        for k in range(1, plane):
            total = total + r1[p, (k - 1) * piece : k * piece, :].astype(F32)
        at2 = core * half + plane_place(0) * piece
        if scattered and p < 4:
            a3[p] = total
            copies = []
            for k in range(1, n_lon):
                there = rows_of(lax.rem(lon + k, n_lon) * strip, strip)
                copies.append(send(a3.at[p, there, :], r3.at[p, k - 1], "lon", k))
            yield
            finish(copies)
            total = a3[p, rows_of(lon * strip, strip), :]
            for k in range(1, n_lon):
                total = total + r3[p, k - 1]
            own = target.at[rows_of(at2 + lon * strip, strip), :]
            own[...] = total.astype(BF16)
            copies = [send(own, own, "lon", k) for k in range(1, n_lon)]
            yield
            finish(copies)
        else:
            near[p, lon] = total.astype(BF16)
            copies = [send(near.at[p, lon], near.at[p, lon], "lon", k) for k in range(1, n_lon)]
            yield
            finish(copies)
            total = near[p, 0].astype(F32)
            for k in range(1, n_lon):
                total = total + near[p, k].astype(F32)
            target[rows_of(at2, piece), :] = total.astype(BF16)
        own = target.at[rows_of(at2, piece), :]
        copies = [send(own, own, "plane", k) for k in range(1, plane)]
        yield
        finish(copies)
        own = target.at[rows_of(core * half, half), :]
        copies = [send(own, own, "core")]
        yield
        finish(copies)
        result = o1_ref if p < 3 else o2_ref
        for n in range(6):
            result[3 * (p % 3) + n // 2, :, (n % 2) * lanes : (n % 2 + 1) * lanes] = full[
                p, n * ch : (n + 1) * ch, :
            ]

    running = {}

    def advance(*parts):
        for p in parts:
            if p in running and next(running[p], "end") == "end":
                del running[p]

    def begin(p, grad):
        running[p] = reduce_steps(p, grad)
        next(running[p])

    edge = jnp.zeros((2 * cols, ch), BF16)
    for z in (gz, bz):
        z[0 : 2 * cols, :] = edge
        z[2 * cols + cells : 4 * cols + cells, :] = edge
    for h in range(rows):
        value = g_ref[h * cols : (h + 1) * cols, :]
        gz[(h + 2) * cols : (h + 3) * cols, :] = value
        gt[:, h * cols : (h + 1) * cols] = value.astype(F32).T.astype(BF16)
    pl.semaphore_wait(barrier, greeted)
    send_field(0, x_ref)
    back_conv(2, gz, w2_ref)

    pad_field(0, x_ref, x1)
    for i in range(2):
        at = slice(i * block, (i + 1) * block)
        value = conv(x1, w1_ref, i)
        sigma = 1.0 / (1.0 + jnp.exp(-value))
        act[at, :] = (value * sigma).astype(BF16)
        slope[at, :] = sigma * (1.0 + value * (1.0 - sigma))
    send_field(1, act)

    halo_wait(2)
    for h in range(rows):
        back = returned_row(2, h) * slope[h * cols : (h + 1) * cols, :]
        bz[(h + 2) * cols : (h + 3) * cols, :] = back.astype(BF16)
        bt[:, h * cols : (h + 1) * cols] = back.T.astype(BF16)

    for r, ready in enumerate(((), (), (0,))):
        begin(r, product(bt[...], x1[r * cols : r * cols + cells, :], NN))
        advance(*ready)
    pad_field(1, act, x2)
    advance(1)
    for r, ready in enumerate(((2,), (), (3,))):
        begin(3 + r, product(gt[...], x2[r * cols : r * cols + cells, :], NN))
        advance(*ready)
    back_conv(3, bz, w1_ref, ((5, 4, 0, 1), (2,)))
    for i, ready in enumerate(((3, 0), (4, 1))):
        at = slice(i * block, (i + 1) * block)
        out_ref[at, :] = (x_ref[at, :].astype(F32) + conv(x2, w2_ref, i)).astype(BF16)
        advance(*ready)
    halo_wait(3)
    for h in range(rows):
        at = slice(h * cols, (h + 1) * cols)
        gf_ref[at, :] = (g_ref[at, :].astype(F32) + returned_row(3, h)).astype(BF16)
    while running:
        advance(*sorted(running, reverse=True))


def per_device(sizes, fields, weight_one, weight_two, edge_flips, cotangent):
    n_lon, n_lat, n_dp = sizes
    _, ch, rows, cols = fields.shape
    cells = rows * cols
    ny = n_dp // 2
    def by_cells(array):
        return jnp.transpose(array[0], (1, 2, 0)).reshape(cells, ch)

    part, half, lanes = 3 * ch, 3 * ch, ch // 2
    piece = half // (ny * n_lat)
    strip = max(8, piece // n_lon)
    copies = 2 * (ny * n_lat + n_lon)
    vmem = pl.BlockSpec(memory_space=pltpu.VMEM)
    padded = ((rows + 2) * cols, part)
    zeroed = ((rows + 4) * cols, ch)
    out, grad_fields, grad_one, grad_two = pl.pallas_call(
        functools.partial(kernel, (n_lon, n_lat, n_dp, rows, cols, ch)),
        out_shape=[jax.ShapeDtypeStruct((cells, ch), BF16)] * 2
        + [jax.ShapeDtypeStruct((9, ch, ch), BF16)] * 2,
        in_specs=[vmem] * 4 + [pl.BlockSpec(memory_space=pltpu.SMEM)],
        out_specs=[vmem] * 4,
        scratch_shapes=[
            pltpu.VMEM(padded, BF16), pltpu.VMEM(padded, BF16),
            pltpu.VMEM(zeroed, BF16), pltpu.VMEM(zeroed, BF16),
            pltpu.VMEM((ch, cells), BF16), pltpu.VMEM((ch, cells), BF16),
            pltpu.VMEM((cells, ch), F32), pltpu.VMEM((cells, ch), F32), pltpu.VMEM((cells, ch), BF16),
            pltpu.VMEM((4, 8, rows, ch), F32), pltpu.VMEM((4, 8, rows, ch), F32),
            pltpu.VMEM((4, 2, cols, ch), BF16), pltpu.VMEM((4, 2, cols, ch), BF16),
            pltpu.VMEM((6, 6 * ch, lanes), F32), pltpu.VMEM((6, half, lanes), F32),
            pltpu.VMEM((6, half, lanes), BF16), pltpu.VMEM((6, half, lanes), F32), pltpu.VMEM((6, half, lanes), BF16),
            pltpu.VMEM((6, piece, lanes), F32), pltpu.VMEM((6, n_lon - 1, strip, lanes), F32),
            pltpu.VMEM((6, n_lon, piece, lanes), BF16), pltpu.VMEM((6, 6 * ch, lanes), BF16),
            pltpu.SemaphoreType.DMA((4, 8)), pltpu.SemaphoreType.DMA((4, 8)),
            pltpu.SemaphoreType.DMA((6, copies)), pltpu.SemaphoreType.DMA((6, copies)),
        ],
        compiler_params=pltpu.CompilerParams(
            collective_id=0, has_side_effects=True, vmem_limit_bytes=52 * 1024 * 1024
        ),
        cost_estimate=pl.CostEstimate(
            flops=12 * 9 * ch * ch * cells, bytes_accessed=8 * 9 * ch * ch, transcendentals=2 * cells * ch
        ),
    )(by_cells(fields), by_cells(cotangent), weight_one, weight_two, edge_flips)

    def by_channels(array):
        return jnp.transpose(array.reshape(rows, cols, ch), (2, 0, 1))[None]

    return (
        by_channels(out),
        by_channels(grad_fields),
        grad_one.astype(F32),
        grad_two.astype(F32),
    )


def solution(mesh):
    tile = P("dp", None, "lat", "lon")
    sizes = tuple(mesh.shape[axis] for axis in ("lon", "lat", "dp"))
    return jax.shard_map(
        functools.partial(per_device, sizes), mesh=mesh,
        in_specs=(tile, P(), P(), P(), tile), out_specs=(tile, tile, P(), P()), check_vma=False,
    )
```
